128 devices in a mesh: space: 16 (over z, y), member: 8 (over x, core).
Axes of the slice: x: 4, y: 4, z: 4, core: 2. Of those that a mesh axis runs over, the one named last changes fastest.
Arguments:
- residual: float32 [512, 512, 512], P('space', 'member'), may hold values from -8 to 8
- mobility: float32 [512, 512, 512], P('space', 'member'), may hold values from 0.1 to 10
- initial_guess: float32 [512, 512, 512], P('space', 'member'), may hold values from -4 to 4
Outputs:
- correction: float32 [512, 512, 512], P('space', 'member')
The draws below stay inside these ranges and needn't reach their ends.
All inputs are finite; a program needn't handle non-finite values.
Results may differ from the reference program's by a relative error of at most 0.00002.
Values sent between devices are 32-bit elements; how exact they have to be, the bound alone decides.
No kernel may reach another device: no remote copies, remote signals or barrier semaphores. Data moves between devices by JAX's collectives and lax.ppermute only.
A program may use at most 192 MiB of HBM per device.

```python
import math
import jax
import jax.numpy as jnp

NX = 512
NY = 512
NZ = 512


def block_levels(stream_key, shape, shards, smallest, top_value):
    level = 1.0
    for dim, parts in shards:
        steps = jax.random.uniform(jax.random.fold_in(jax.random.fold_in(stream_key, 6), dim), (parts,), jnp.float32, smallest / len(shards), top_value / len(shards))
        level = level * jnp.repeat(jnp.exp(steps), shape[dim] // parts).reshape((-1,) + (1,) * (len(shape) - 1 - dim))
    return level


def centred(key, extent, spread, reach, shards=(), dtype=jnp.bfloat16):
    gain = block_levels(key, extent, shards, -0.22, 0.18) if shards else 1.0
    result = jax.random.normal(key, extent, jnp.float32) * spread * gain
    return jnp.minimum(jnp.maximum(result, -reach), reach).astype(dtype)


def setup_inputs(seed: int = 0) -> dict:
    streams_of = jax.random.split(jax.random.key(seed), 4)
    residual = centred(streams_of[0], (NX, NY, NZ), 1.0, 8.0, ((0, 16), (1, 8)), jnp.float32)
    mobility = jnp.clip(jnp.exp(math.log(10.0) - 4.6051702 * jax.random.uniform(streams_of[1], (NX, NY, NZ), jnp.float32) ** block_levels(streams_of[1], (NX, NY, NZ), ((0, 16), (1, 8)), -0.2, 0.2)), 0.1, 10.0)
    initial_guess = centred(streams_of[2], (NX, NY, NZ), 0.5, 4.0, ((0, 16), (1, 8)), jnp.float32)
    return {"residual": residual, "mobility": mobility, "initial_guess": initial_guess}


sweep_weights = tuple(1.0 / (1.15 + 0.85 * math.cos(math.pi * (2 * j - 1) / 4.0)) for j in (1, 2))


def neighbours(padded):
    return [padded[2:, 1:-1, 1:-1], padded[:-2, 1:-1, 1:-1],
            padded[1:-1, 2:, 1:-1], padded[1:-1, :-2, 1:-1],
            padded[1:-1, 1:-1, 2:], padded[1:-1, 1:-1, :-2]]


def face_terms(padded_mob):
    center = padded_mob[1:-1, 1:-1, 1:-1]
    return [0.5 * (center + other) for other in neighbours(padded_mob)]


def sweep(padded_field, field, rhs, coeffs, diag, weight):
    flux = jnp.zeros_like(field)
    for coef, other in zip(coeffs, neighbours(padded_field)):
        flux = flux + coef * other
    image = diag * field - flux
    return field + weight * (rhs - image) / diag


def reference(residual, mobility, initial_guess):
    coeffs = face_terms(jnp.pad(mobility, 1))
    diag = coeffs[0] + coeffs[1] + coeffs[2] + coeffs[3] + coeffs[4] + coeffs[5]
    field = initial_guess
    for weight in sweep_weights:
        field = sweep(jnp.pad(field, 1), field, residual, coeffs, diag, weight)
    return field
```

```python
import math

import jax
import jax.numpy as jnp
from jax import lax
from jax.experimental import pallas as pl
from jax.experimental.pallas import tpu as pltpu
from jax.sharding import PartitionSpec as P

sweep_weights = tuple((1.0 / (1.15 + 0.85 * math.cos(math.pi * (2 * j - 1) / 4.0)) for j in (1, 2)))

LANES = 128
RING = 4
ROWS = 8
VMEM = pl.BlockSpec(memory_space=pltpu.VMEM)
HBM = pl.BlockSpec(memory_space=pltpu.HBM)
F32 = jnp.float32


def lane_slices(nz):
    return [slice(k * LANES, (k + 1) * LANES) for k in range(nz // LANES)]


def iotas():
    row = lax.broadcasted_iota(jnp.int32, (ROWS, LANES), 0)
    lane = lax.broadcasted_iota(jnp.int32, (ROWS, LANES), 1)
    return row, lane


class Slab:
    def __init__(self, fields, rings, row_ok):
        self.e, self.m, self.r = fields
        self.cx, self.cy, self.cz, self.rt, self.e1 = rings
        self.strips = self.cx.shape[1] // ROWS - 1
        self.tiles = lane_slices(self.cx.shape[2])
        self.row_ok = row_ok
        row, lane = iotas()
        self.first_row, self.last_row = row == 0, row == ROWS - 1
        self.first_lane, self.last_lane = lane == 0, lane == LANES - 1

    def slot(self, i):
        return (i + RING) % RING if isinstance(i, int) else lax.rem(i, RING)

    def get(self, field, i, j):
        plane, halo = field(i)
        ref, at = halo if j == self.strips else plane
        first = 0 if j == self.strips else ROWS * j
        return [ref[at, first : first + ROWS, s] for s in self.tiles]

    def ring(self, ref, i, j):
        return [ref[i, ROWS * j : ROWS * (j + 1), s] for s in self.tiles]

    def put(self, ref, i, j, vals):
        for s, v in zip(self.tiles, vals):
            ref[i, ROWS * j : ROWS * (j + 1), s] = v

    def roll_up(self, vals):
        return [pltpu.roll(v, ROWS - 1, 0) for v in vals]

    def roll_down(self, vals):
        return [pltpu.roll(v, 1, 0) for v in vals]

    def next_rows(self, here, there):
        return [jnp.where(self.last_row, b, a) for a, b in zip(here, there)]

    def prev_rows(self, here, there):
        return [jnp.where(self.first_row, b, a) for a, b in zip(here, there)]

    def next_lanes(self, vals):
        turned = [pltpu.roll(v, LANES - 1, 1) for v in vals]
        return [jnp.where(self.last_lane, b, a) for a, b in zip(turned, turned[1:] + [0.0])]

    def prev_lanes(self, vals):
        turned = [pltpu.roll(v, 1, 1) for v in vals]
        return [jnp.where(self.first_lane, b, a) for a, b in zip(turned, [0.0] + turned[:-1])]

    def first(self, i, halo_strip=True, keep=None):
        w = sweep_weights[0]
        n = self.strips
        last = n if halo_strip else n - 1
        cur, prev = self.slot(i), self.slot(i - 1)

        def load(j):
            e = self.get(self.e, i, j)
            m = self.get(self.m, i, j)
            return e, m, self.roll_up(e), self.roll_up(m), [f(v) for v in (e, m) for f in (self.next_lanes, self.prev_lanes)]

        e, m = self.get(self.e, i, n), self.get(self.m, i, n)
        top = here = load(0)
        cy = [a + b for a, b in zip(m, self.next_rows(self.roll_up(m), top[3]))]
        cyd = self.roll_down(cy)
        gd = self.roll_down([a * b for a, b in zip(cy, e)])
        for j in range(last + 1):
            there = load(j + 1) if j < n else top
            e, m, eu, mu, (e_zp, e_zm, m_zp, m_zm) = here
            cy = [a + b for a, b in zip(m, self.next_rows(mu, there[3]))]
            cyd_j = self.roll_down(cy)
            gd_j = self.roll_down([a * b for a, b in zip(cy, e)])
            cy_dn, g_dn = self.prev_rows(cyd_j, cyd), self.prev_rows(gd_j, gd)
            e_up = self.next_rows(eu, there[2])
            exm = self.get(self.e, i - 1, j)
            exp = self.get(self.e, i + 1, j)
            mxp = self.get(self.m, i + 1, j)
            r = self.get(self.r, i, j)
            cxm = self.ring(self.cx, prev, j)
            keeps = [[], [], [], [], []]
            for k in range(len(self.tiles)):
                cx = m[k] + mxp[k]
                cz, cz_dn = m[k] + m_zp[k], m[k] + m_zm[k]
                t = ((cx + cxm[k]) + (cy[k] + cy_dn[k])) + (cz + cz_dn)
                num = ((cx * exp[k] + cxm[k] * exm[k]) + (cy[k] * e_up[k] + g_dn[k])) + (
                    (cz * e_zp[k] + cz_dn * e_zm[k]) + (r[k] + r[k])
                )
                rt = 1.0 / t
                e1 = (1.0 - w) * e[k] + (w * rt) * num
                if j == n:
                    e1 = jnp.where(self.row_ok, e1, 0.0)
                if keep is not None:
                    e1 = jnp.where(keep, e1, 0.0)
                for vals, v in zip(keeps, (cx, cy[k], cz, rt, e1)):
                    vals.append(v)
            for ref, vals in zip((self.cx, self.cy, self.cz, self.rt, self.e1), keeps):
                if j < n or ref is self.cx or ref is self.cy or ref is self.e1:
                    self.put(ref, cur, j, vals)
            cyd, gd = cyd_j, gd_j
            here = there
            yield

    def faces_x(self, i, strips):
        for j in strips:
            m = self.get(self.m, i, j)
            mxp = self.get(self.m, i + 1, j)
            self.put(self.cx, self.slot(i), j, [a + b for a, b in zip(m, mxp)])

    def second(self, i, out, o):
        w = sweep_weights[1]
        n = self.strips
        cur, prev, nxt = self.slot(i), self.slot(i - 1), self.slot(i + 1)

        def load(j):
            e, cy = self.ring(self.e1, cur, j), self.ring(self.cy, cur, j)
            g = self.roll_down([a * b for a, b in zip(cy, e)])
            if j == n:
                return e, cy, g, self.roll_up(e)
            cz = self.ring(self.cz, cur, j)
            h = self.prev_lanes([a * b for a, b in zip(cz, e)])
            return e, cy, g, self.roll_up(e), cz, self.next_lanes(e), h

        gd = load(n)[2]
        here = load(0)
        for j in range(n):
            there = load(j + 1)
            e, cy, g, eu, cz, e_zp, h_dn = here
            e_up, g_dn = self.next_rows(eu, there[3]), self.prev_rows(g, gd)
            exm, exp = self.ring(self.e1, prev, j), self.ring(self.e1, nxt, j)
            cxm, cx = self.ring(self.cx, prev, j), self.ring(self.cx, cur, j)
            rt = self.ring(self.rt, cur, j)
            r = self.get(self.r, i, j)
            outs = []
            for k in range(len(self.tiles)):
                num = ((cx[k] * exp[k] + cxm[k] * exm[k]) + (cy[k] * e_up[k] + g_dn[k])) + (
                    (cz[k] * e_zp[k] + h_dn[k]) + (r[k] + r[k])
                )
                outs.append((1.0 - w) * e[k] + (w * rt[k]) * num)
            self.put(out, o, j, outs)
            here, gd = there, g
            yield


def run(*passes):
    passes = list(passes)
    while passes:
        passes = [p for p in passes if next(p, StopIteration) is not StopIteration]


def pairs(first, n):
    return [p for i in range(first, n - 1, 2) for p in ((i, i + 1), (i + 1, i))]


def is_even(axis):
    return lax.rem(lax.axis_index(axis), 2) == 0


def swap(x, axis, first):
    return lax.ppermute(x, axis, pairs(first, lax.axis_size(axis)))


def row_mask():
    me, last = lax.axis_index("member"), lax.axis_size("member") - 1
    row, _ = iotas()
    after = jnp.where(me < last, 1, 0)
    before = jnp.where(me > 0, 1, 0)
    return jnp.where(row < ROWS // 2, after, before) == 1


def rings(ny, nz):
    return [pltpu.VMEM((RING, ny + ROWS, nz), F32)] * 5


def turned(v, by):
    return pltpu.roll(v, by % ROWS, 0)


def send_kernel(e, m, r, to_row_even, to_row_odd, to_plane_even, to_plane_odd, top, bottom, sems, plane_sems):
    nx, ny, nz = e.shape
    reads = []
    for k, src in enumerate((e, m, r)):
        for dst, at in ((top, 0), (bottom, ny - ROWS)):
            reads.append(pltpu.make_async_copy(src.at[:, at : at + ROWS], dst.at[k], sems.at[len(reads)]))
    for c in reads:
        c.start()
    even = is_even("space")
    planes = []
    for dst, high in ((to_plane_even, even), (to_plane_odd, jnp.logical_not(even))):
        two, one = jnp.where(high, nx - 2, 0), jnp.where(high, nx - 1, 0)
        for src, dst_at, size, at in ((e, 0, 2, two), (m, 2, 2, two), (r, 4, 1, one)):
            planes.append(
                pltpu.make_async_copy(src.at[pl.ds(at, size)], dst.at[dst_at : dst_at + size], plane_sems.at[len(planes)])
            )
    for c in planes:
        c.start()
    for c in reads:
        c.wait()

    def fill(to_next, to_prev):
        row = lax.broadcasted_iota(jnp.int32, (ROWS, nz), 0)

        @pl.loop(0, nx)
        def _(i):
            to_next[i] = jnp.where(
                row >= ROWS - 2,
                bottom[0, i],
                jnp.where(row >= ROWS - 4, turned(bottom[1, i], -2), turned(bottom[2, i], -4)),
            )
            to_prev[i] = jnp.where(row < 2, top[0, i], jnp.where(row < 4, turned(top[1, i], 2), turned(top[2, i], 4)))

    @pl.when(is_even("member"))
    def _():
        fill(to_row_even, to_row_odd)

    @pl.when(jnp.logical_not(is_even("member")))
    def _():
        fill(to_row_odd, to_row_even)

    for c in planes:
        c.wait()


def send(e, m, r):
    nx, ny, nz = e.shape
    rows = jax.ShapeDtypeStruct((nx, ROWS, nz), F32)
    planes = jax.ShapeDtypeStruct((5, ny, nz), F32)
    strips = pltpu.VMEM((3, nx, ROWS, nz), F32)
    return pl.pallas_call(
        send_kernel,
        out_shape=[rows, rows, planes, planes],
        in_specs=[HBM] * 3,
        out_specs=[VMEM] * 4,
        scratch_shapes=[strips, strips, pltpu.SemaphoreType.DMA((6,)), pltpu.SemaphoreType.DMA((6,))],
        compiler_params=pltpu.CompilerParams(vmem_limit_bytes=16 * 2**20),
        name="send",
    )(e, m, r)


def halo_kernel(got_even, got_odd, eh, mh, rh, corner_even, corner_odd):
    nx, _, nz = eh.shape
    row = lax.broadcasted_iota(jnp.int32, (ROWS, nz), 0)
    after = row < ROWS // 2

    def fill(from_next, from_prev):
        @pl.loop(0, nx)
        def _(i):
            a, b = from_next[i], from_prev[i]
            eh[i] = jnp.where(after, a, b)
            mh[i] = jnp.where(after, turned(a, -2), turned(b, 2))
            rh[i] = jnp.where(after, turned(a, -4), turned(b, 4))

    @pl.when(is_even("member"))
    def _():
        fill(got_even, got_odd)

    @pl.when(jnp.logical_not(is_even("member")))
    def _():
        fill(got_odd, got_even)

    even = is_even("space")
    for dst, high in ((corner_even, even), (corner_odd, jnp.logical_not(even))):
        at = jnp.where(high, nx - 1, 0)
        dst[0] = eh[at]
        dst[1] = mh[at]


def halo(got_even, got_odd):
    nx, _, nz = got_even.shape
    strip = jax.ShapeDtypeStruct((nx, ROWS, nz), F32)
    corner = jax.ShapeDtypeStruct((2, ROWS, nz), F32)
    return pl.pallas_call(
        halo_kernel,
        out_shape=[strip] * 3 + [corner] * 2,
        in_specs=[VMEM] * 2,
        out_specs=[VMEM] * 5,
        compiler_params=pltpu.CompilerParams(vmem_limit_bytes=8 * 2**20),
        name="halo",
    )(got_even, got_odd)


def inner_kernel(e, m, r, eh, mh, rh, out_hbm, out, cx, cy, cz, rt, e1, sems):
    nx = e.shape[0]
    fields = [lambda i, own=own, strip=strip: ((own, i), (strip, i)) for own, strip in ((e, eh), (m, mh), (r, rh))]
    slab = Slab(fields, (cx, cy, cz, rt, e1), row_mask())

    def out_copy(i):
        return pltpu.make_async_copy(out.at[i], out_hbm.at[i], sems.at[i])

    slab.faces_x(0, range(slab.strips + 1))

    @pl.loop(1, 4)
    def _(i):
        run(slab.first(i))

    @pl.loop(4, nx - 1)
    def _(i):
        run(slab.second(i - 2, out, i - 2), slab.first(i))
        out_copy(i - 2).start()

    run(slab.second(nx - 3, out, nx - 3))
    out_copy(nx - 3).start()

    @pl.loop(2, nx - 2)
    def _(i):
        out_copy(i).wait()


def inner(e, m, r, eh, mh, rh):
    nx, ny, nz = e.shape
    return pl.pallas_call(
        inner_kernel,
        out_shape=jax.ShapeDtypeStruct((nx, ny, nz), F32),
        in_specs=[VMEM] * 6,
        out_specs=HBM,
        scratch_shapes=[pltpu.VMEM((nx, ny, nz), F32)] + rings(ny, nz) + [pltpu.SemaphoreType.DMA((nx,))],
        compiler_params=pltpu.CompilerParams(vmem_limit_bytes=16 * 2**20),
        cost_estimate=pl.CostEstimate(flops=70 * nx * ny * nz, bytes_accessed=16 * nx * ny * nz, transcendentals=0),
        name="inner",
    )(e, m, r, eh, mh, rh)


def outer_kernel(e, m, r, eh, mh, rh, got_even, got_odd, corner_even, corner_odd, _, out_hbm, out, cx, cy, cz, rt, e1, sems):
    nx = e.shape[0]
    me, count = lax.axis_index("space"), lax.axis_size("space")
    mask = row_mask()
    writes = []
    for side, (got, corner) in enumerate(((got_even, corner_even), (got_odd, corner_odd))):
        high = is_even("space") if side == 0 else jnp.logical_not(is_even("space"))

        def at(q, high=high):
            return jnp.where(high, nx - 1 - q, q)

        def field(k, own, strip, got=got, corner=corner, high=high, at=at):
            def find(q):
                if q >= 0:
                    return (own, at(q)), (strip, at(q))
                if k == 2:
                    return (got, 4), None
                return (got, 2 * k + jnp.where(high, -1 - q, 2 + q)), (corner, k)

            return find

        fields = [field(k, *refs) for k, refs in enumerate(((e, eh), (m, mh), (r, rh)))]
        slab = Slab(fields, (cx, cy, cz, rt, e1), mask)
        there = jnp.where(high, me < count - 1, me > 0)
        keep = jnp.broadcast_to(jnp.where(there, 1, 0), (ROWS, LANES)) == 1
        slab.faces_x(-2, range(slab.strips))
        slab.faces_x(-1, [slab.strips])
        run(slab.first(-1, halo_strip=False, keep=keep))
        run(slab.first(0))
        run(slab.first(1))
        run(slab.first(2))
        for q in (0, 1):
            run(slab.second(q, out, 2 * side + q))
            c = pltpu.make_async_copy(out.at[2 * side + q], out_hbm.at[at(q)], sems.at[2 * side + q])
            c.start()
            writes.append(c)
    for c in writes:
        c.wait()


def outer(e, m, r, eh, mh, rh, got_even, got_odd, corner_even, corner_odd, out):
    nx, ny, nz = e.shape
    return pl.pallas_call(
        outer_kernel,
        out_shape=jax.ShapeDtypeStruct((nx, ny, nz), F32),
        in_specs=[VMEM] * 10 + [HBM],
        out_specs=HBM,
        input_output_aliases={10: 0},
        scratch_shapes=[pltpu.VMEM((4, ny, nz), F32)] + rings(ny, nz) + [pltpu.SemaphoreType.DMA((4,))],
        compiler_params=pltpu.CompilerParams(vmem_limit_bytes=16 * 2**20),
        name="outer",
    )(e, m, r, eh, mh, rh, got_even, got_odd, corner_even, corner_odd, out)


def shards(residual, mobility, initial_guess):
    e, m, r = initial_guess, mobility, residual
    row_even, row_odd, plane_even, plane_odd = send(e, m, r)
    row_even = swap(row_even, "member", 0)
    row_odd = swap(row_odd, "member", 1)
    plane_even = swap(plane_even, "space", 0)
    plane_odd = swap(plane_odd, "space", 1)
    eh, mh, rh, corner_even, corner_odd = halo(row_even, row_odd)
    corner_even = swap(corner_even, "space", 0)
    corner_odd = swap(corner_odd, "space", 1)
    out = inner(e, m, r, eh, mh, rh)
    return outer(e, m, r, eh, mh, rh, plane_even, plane_odd, corner_even, corner_odd, out)


def solution(mesh):
    placed = P("space", "member", None)
    return jax.shard_map(shards, mesh=mesh, in_specs=(placed,) * 3, out_specs=placed, check_vma=False)
```

```python
import math

import jax
import jax.numpy as jnp
from jax import lax
from jax.experimental import pallas as pl
from jax.experimental.pallas import tpu as pltpu
from jax.sharding import PartitionSpec as P

sweep_weights = tuple((1.0 / (1.15 + 0.85 * math.cos(math.pi * (2 * j - 1) / 4.0)) for j in (1, 2)))

LANES = 128
ROWS = 8
VMEM = pl.BlockSpec(memory_space=pltpu.VMEM)
HBM = pl.BlockSpec(memory_space=pltpu.HBM)
F32 = jnp.float32


def lane_slices(nz):
    return [slice(k * LANES, (k + 1) * LANES) for k in range(nz // LANES)]


def iotas():
    row = lax.broadcasted_iota(jnp.int32, (ROWS, LANES), 0)
    lane = lax.broadcasted_iota(jnp.int32, (ROWS, LANES), 1)
    return row, lane


def next_lanes(vals, last_lane):
    turned = [pltpu.roll(v, LANES - 1, 1) for v in vals]
    return [jnp.where(last_lane, b, a) for a, b in zip(turned, turned[1:] + [0.0])]


def prev_lanes(vals, first_lane):
    turned = [pltpu.roll(v, 1, 1) for v in vals]
    return [jnp.where(first_lane, b, a) for a, b in zip(turned, [0.0] + turned[:-1])]


class Slab:
    def __init__(self, place, turning, ny, nz, row_ok):
        self.place, self.turning = place, turning
        self.strips = ny // ROWS
        self.tiles = lane_slices(nz)
        self.row_ok = row_ok
        _, lane = iotas()
        self.first_lane, self.last_lane = lane == 0, lane == LANES - 1

    def get(self, name, i, j):
        ref, at, row = self.place(name, i, j)
        return [ref[at, row : row + ROWS, s] for s in self.tiles]

    def put(self, name, i, j, vals):
        ref, at, row = self.place(name, i, j)
        for s, v in zip(self.tiles, vals):
            ref[at, row : row + ROWS, s] = v

    def load(self, i, strips, names):
        for j in strips:
            for name in names:
                ref, at = self.turning(name, i)
                vals = self.get(name, i, j)
                for row in (0, ROWS * (j + 1)) if j == self.strips else (ROWS * (j + 1),):
                    for k, v in enumerate(vals):
                        ref[at, k, row : row + ROWS, :] = v
            yield

    def shifted(self, name, i, j, by=0):
        ref, at = self.turning(name, i)
        if j == self.strips:
            row = {0: 0, 1: 1, -1: ROWS * (j + 1) - 1}[by]
        else:
            row = ROWS * (j + 1) + by
        return [ref[at, k, row : row + ROWS, :] for k in range(len(self.tiles))]

    def first(self, i, strips, keep=None):
        w = sweep_weights[0]
        n = self.strips
        strips = list(strips)

        def ahead(j):
            e, m = self.shifted("e", i, j), self.shifted("m", i, j)
            return (
                e,
                m,
                next_lanes(e, self.last_lane),
                prev_lanes(e, self.first_lane),
                next_lanes(m, self.last_lane),
                prev_lanes(m, self.first_lane),
            )

        here = ahead(strips[0])
        for j, after in zip(strips, strips[1:] + [None]):
            there = None if after is None else ahead(after)
            e, m, e_zp, e_zm, m_zp, m_zm = here
            e_up, e_dn = self.shifted("e", i, j, 1), self.shifted("e", i, j, -1)
            m_up, m_dn = self.shifted("m", i, j, 1), self.shifted("m", i, j, -1)
            e_xp, e_xm = self.get("e", i + 1, j), self.get("e", i - 1, j)
            m_xp, m_xm = self.get("m", i + 1, j), self.get("m", i - 1, j)
            r = self.get("r", i, j)
            made = []
            for k in range(len(self.tiles)):
                cx, cxm = m[k] + m_xp[k], m[k] + m_xm[k]
                cy, cy_dn = m[k] + m_up[k], m[k] + m_dn[k]
                cz, cz_dn = m[k] + m_zp[k], m[k] + m_zm[k]
                t = ((cx + cxm) + (cy + cy_dn)) + (cz + cz_dn)
                num = ((cx * e_xp[k] + cxm * e_xm[k]) + (cy * e_up[k] + cy_dn * e_dn[k])) + (
                    (cz * e_zp[k] + cz_dn * e_zm[k]) + (r[k] + r[k])
                )
                rt = 1.0 / t
                e1 = (1.0 - w) * e[k] + (w * rt) * num
                if j == n:
                    e1 = jnp.where(self.row_ok, e1, 0.0)
                if keep is not None:
                    e1 = jnp.where(keep, e1, 0.0)
                made.append((cx, cy, cz, rt, e1))
            cx, cy, cz, rt, e1 = zip(*made)
            self.put("cy", i, j, cy)
            self.put("e1", i, j, e1)
            if j < n:
                self.put("cx", i, j, cx)
                self.put("cz", i, j, cz)
                self.put("rt", i, j, rt)
            here = there
            yield

    def second(self, i, out, o):
        w = sweep_weights[1]

        def ahead(j):
            e, cz = self.shifted("e1", i, j), self.get("cz", i, j)
            return e, cz, next_lanes(e, self.last_lane), prev_lanes([a * b for a, b in zip(cz, e)], self.first_lane)

        here = ahead(0)
        for j in range(self.strips):
            there = ahead(j + 1) if j < self.strips - 1 else None
            e, cz, e_zp, h_dn = here
            e_up, e_dn = self.shifted("e1", i, j, 1), self.shifted("e1", i, j, -1)
            cy, cy_dn = self.shifted("cy", i, j), self.shifted("cy", i, j, -1)
            e_xp, e_xm = self.get("e1", i + 1, j), self.get("e1", i - 1, j)
            cx, cxm = self.get("cx", i, j), self.get("cx", i - 1, j)
            rt = self.get("rt", i, j)
            r = self.get("r", i, j)
            outs = []
            for k in range(len(self.tiles)):
                num = ((cx[k] * e_xp[k] + cxm[k] * e_xm[k]) + (cy[k] * e_up[k] + cy_dn[k] * e_dn[k])) + (
                    (cz[k] * e_zp[k] + h_dn[k]) + (r[k] + r[k])
                )
                outs.append((1.0 - w) * e[k] + (w * rt[k]) * num)
            for s, v in zip(self.tiles, outs):
                out[o, ROWS * j : ROWS * (j + 1), s] = v
            here = there
            yield


def run(*passes):
    passes = list(passes)
    while passes:
        passes = [p for p in passes if next(p, StopIteration) is not StopIteration]


RING1, RING2 = 6, 4
TURNED1, TURNED2 = ("e", "m"), ("e1", "cy")
MADE = ("e1", "cy", "cx", "cz", "rt")


def turned_shape(planes, ny, nz):
    return (planes, nz // LANES, ny + 2 * ROWS, LANES)


class Plane:
    def __init__(self, number, slot):
        self.number, self.slot = number, slot

    def __add__(self, by):
        return self.number + by

    def __sub__(self, by):
        return self.number - by


def number(i):
    return i.number if isinstance(i, Plane) else i


def ringed(first, last, size, ahead, body):
    @pl.loop(0, (last - first + 1) // size)
    def _(t):
        for k in range(size):
            i = first + size * t + k
            body(Plane(i, k), Plane(jnp.minimum(i + ahead, last), (k + ahead) % size))


def along_space(x, back):
    ns, nm = lax.axis_size("space"), lax.axis_size("member")
    hops = []
    for m in range(nm):
        step = 1 if m % 2 == 0 else -1
        for i in range(ns):
            to = (i + step, m) if 0 <= i + step < ns else (i, m + step)
            hops.append((i * nm + m, to[0] * nm + to[1]))
    return lax.ppermute(x, ("space", "member"), [(b, a) for a, b in hops] if back else hops)


def along_member(x, back):
    n = lax.axis_size("member")
    return lax.ppermute(x, "member", [((i + 1) % n, i) if back else (i, (i + 1) % n) for i in range(n)])


def sends_up(back):
    even = lax.rem(lax.axis_index("member"), 2) == 0
    return jnp.logical_not(even) if back else even


def has_next(axis):
    return lax.axis_index(axis) < lax.axis_size(axis) - 1


def has_prev(axis):
    return lax.axis_index(axis) > 0


def row_mask():
    row, _ = iotas()
    after, before = jnp.where(has_next("member"), 1, 0), jnp.where(has_prev("member"), 1, 0)
    return jnp.where(row < ROWS // 2, after, before) == 1


def send_kernel(e, m, r, to_next, to_prev, plane_out, plane_back, top, bottom, sems, plane_sems):
    nx, ny, nz = e.shape
    groups = nx // ROWS
    planes = []
    for dst, back in ((plane_out, False), (plane_back, True)):
        up = sends_up(back)
        two, one = jnp.where(up, nx - 2, 0), jnp.where(up, nx - 1, 0)
        for src, dst_at, size, at in ((e, 0, 2, two), (m, 2, 2, two), (r, 4, 1, one)):
            planes.append(
                pltpu.make_async_copy(src.at[pl.ds(at, size)], dst.at[dst_at : dst_at + size], plane_sems.at[len(planes)])
            )
    for c in planes:
        c.start()
    reads = []
    for k, src in enumerate((e, m, r)):
        for dst, at in ((top, 0), (bottom, ny - ROWS)):
            reads.append(pltpu.make_async_copy(src.at[:, at : at + ROWS], dst.at[k], sems.at[len(reads)]))
    for c in reads:
        c.start()
    for c in planes:
        c.wait()
    for dst, back in ((plane_out, False), (plane_back, True)):

        @pl.when(jnp.logical_not(jnp.where(sends_up(back), has_next("space"), has_prev("space"))))
        def _(dst=dst):
            dst[...] = jnp.zeros_like(dst)

    for c in reads:
        c.wait()
    next_ok, prev_ok = has_next("member"), has_prev("member")
    for n, (k, below, above) in enumerate(((0, 2, 0), (0, 1, 1), (1, 2, 0), (1, 1, 1), (2, 1, 0))):
        for g in range(groups):
            at = slice(ROWS * g, ROWS * (g + 1))
            to_next[groups * n + g] = jnp.where(next_ok, bottom[k, at, ROWS - below, :], 0.0)
            to_prev[groups * n + g] = jnp.where(prev_ok, top[k, at, above, :], 0.0)


def send(e, m, r):
    nx, ny, nz = e.shape
    rows = jax.ShapeDtypeStruct((5 * (nx // ROWS), ROWS, nz), F32)
    planes = jax.ShapeDtypeStruct((5, ny, nz), F32)
    strips = pltpu.VMEM((3, nx, ROWS, nz), F32)
    return pl.pallas_call(
        send_kernel,
        out_shape=[rows, rows, planes, planes],
        in_specs=[HBM] * 3,
        out_specs=[VMEM] * 4,
        scratch_shapes=[strips, strips, pltpu.SemaphoreType.DMA((6,)), pltpu.SemaphoreType.DMA((6,))],
        compiler_params=pltpu.CompilerParams(vmem_limit_bytes=8 * 2**20),
        name="send",
    )(e, m, r)


def halo_kernel(from_prev, from_next, _, eh, mh, rh, corner_out, corner_back):
    nx, _, nz = eh.shape
    groups = nx // ROWS
    for ref in (eh, mh, rh):
        ref[...] = jnp.zeros_like(ref)
    for n, (ref, below, above) in enumerate(((eh, 2, 0), (eh, 1, 1), (mh, 2, 0), (mh, 1, 1), (rh, 1, 0))):
        for g in range(groups):
            at = slice(ROWS * g, ROWS * (g + 1))
            ref[at, ROWS - below, :] = from_prev[groups * n + g]
            ref[at, above, :] = from_next[groups * n + g]
    for dst, back in ((corner_out, False), (corner_back, True)):
        up = sends_up(back)
        ok = jnp.where(up, has_next("space"), has_prev("space"))
        at = jnp.where(up, nx - 1, 0)
        dst[0] = jnp.where(ok, eh[at], 0.0)
        dst[1] = jnp.where(ok, mh[at], 0.0)


def halo(from_prev, from_next, nx, after):
    nz = from_prev.shape[2]
    strip = jax.ShapeDtypeStruct((nx, ROWS, nz), F32)
    corner = jax.ShapeDtypeStruct((2, ROWS, nz), F32)
    return pl.pallas_call(
        halo_kernel,
        out_shape=[strip] * 3 + [corner] * 2,
        in_specs=[VMEM] * 2 + [pl.BlockSpec(memory_space=pl.ANY)],
        out_specs=[VMEM] * 5,
        compiler_params=pltpu.CompilerParams(vmem_limit_bytes=2 * 2**20),
        name="halo",
    )(from_prev, from_next, after)


def middle_kernel(e, m, r, *rest):
    nx, ny, nz = e.shape
    arrays = dict(zip(("e", "m", "r") + MADE, (e, m, r) + rest))
    rings = dict(zip(TURNED1, rest[len(MADE) :]))
    slab = Slab(
        lambda name, i, j: (arrays[name], number(i), ROWS * j), lambda name, i: (rings[name], i.slot), ny, nz, None
    )
    strips = range(slab.strips)
    for k in range(RING1 // 2):
        run(slab.load(Plane(1 + k, k), strips, TURNED1))
    ringed(
        1,
        nx - 2,
        RING1,
        RING1 // 2,
        lambda i, later: run(slab.first(i, strips[1:-1]), slab.load(later, strips, TURNED1)),
    )


def middle(own):
    nx, ny, nz = own[0].shape
    return pl.pallas_call(
        middle_kernel,
        out_shape=[jax.ShapeDtypeStruct((nx, ny, nz), F32)] * len(MADE),
        in_specs=[VMEM] * 3,
        out_specs=[VMEM] * len(MADE),
        scratch_shapes=[pltpu.VMEM(turned_shape(RING1, ny, nz), F32)] * 2,
        compiler_params=pltpu.CompilerParams(vmem_limit_bytes=4 * 2**20),
        cost_estimate=pl.CostEstimate(flops=40 * nx * ny * nz, bytes_accessed=16 * nx * ny * nz, transcendentals=0),
        name="middle",
    )(*own)


def made_place(middles, ends, n, name, i, j):
    if 0 < j < n - 1:
        return middles[name], i, ROWS * j
    return ends[name], i, ROWS * {0: 0, n - 1: 1, n: 2}[j]


def inner_kernel(e, m, r, eh, mh, rh, *rest):
    nx, ny, nz = e.shape
    n = ny // ROWS
    own = {"e": (e, eh), "m": (m, mh), "r": (r, rh)}
    middles, rest = dict(zip(MADE, rest)), rest[len(MADE) :]
    out_hbm, ends, rest = rest[0], dict(zip(MADE, rest[1:])), rest[1 + len(MADE) :]
    rings, (out, sems) = dict(zip(TURNED1 + TURNED2, rest)), rest[4:]

    def place(name, i, j):
        if name in own:
            ref, strip = own[name]
            return (strip, number(i), 0) if j == n else (ref, number(i), ROWS * j)
        return made_place(middles, ends, n, name, number(i), j)

    slab = Slab(place, lambda name, i: (rings[name], i.slot), ny, nz, row_mask())

    def out_copy(i):
        return pltpu.make_async_copy(out.at[i], out_hbm.at[i], sems.at[i])

    around = [0, 1, n - 2, n - 1, n]
    for k in range(RING1 // 2):
        run(slab.load(Plane(1 + k, k), around, TURNED1))
    ringed(
        1,
        nx - 2,
        RING1,
        RING1 // 2,
        lambda i, later: run(slab.first(i, [0, n - 1, n]), slab.load(later, around, TURNED1)),
    )
    for k in range(RING2 // 2):
        run(slab.load(Plane(2 + k, k), range(n + 1), TURNED2))

    def step(i, later):
        run(slab.second(i, out, number(i)), slab.load(later, range(n + 1), TURNED2))
        out_copy(number(i)).start()

    ringed(2, nx - 3, RING2, RING2 // 2, step)

    @pl.loop(2, nx - 2)
    def _(i):
        out_copy(i).wait()


def inner(own, strips, middles):
    nx, ny, nz = own[0].shape
    args = (*own, *strips, *middles)
    return pl.pallas_call(
        inner_kernel,
        out_shape=[jax.ShapeDtypeStruct((nx, ny, nz), F32)] + [jax.ShapeDtypeStruct((nx, 3 * ROWS, nz), F32)] * len(MADE),
        in_specs=[VMEM] * len(args),
        out_specs=[HBM] + [VMEM] * len(MADE),
        scratch_shapes=[pltpu.VMEM(turned_shape(RING1, ny, nz), F32)] * 2
        + [pltpu.VMEM(turned_shape(RING2, ny, nz), F32)] * 2
        + [pltpu.VMEM((nx, ny, nz), F32), pltpu.SemaphoreType.DMA((nx,))],
        compiler_params=pltpu.CompilerParams(vmem_limit_bytes=9 * 2**20),
        cost_estimate=pl.CostEstimate(flops=40 * nx * ny * nz, bytes_accessed=16 * nx * ny * nz, transcendentals=0),
        name="inner",
    )(*args)


def outer_kernel(e, m, r, eh, mh, rh, got_out, got_back, corner_out, corner_back, *rest):
    nx, ny, nz = e.shape
    n = ny // ROWS
    count = len(MADE)
    middles, ends, rest = dict(zip(MADE, rest)), dict(zip(MADE, rest[count:])), rest[2 * count + 1 :]
    out_hbm, made, rest = rest[0], dict(zip(MADE, rest[1:])), rest[1 + count :]
    rings, (out, sems) = dict(zip(TURNED1 + TURNED2, rest)), rest[4:]
    own = {"e": e, "m": m, "r": r}
    strips = {"e": eh, "m": mh, "r": rh}
    got_at = {"e": 0, "m": 2}
    corner_at = {"e": 0, "m": 1}
    mask = row_mask()
    writes = []
    for side, (got, corner) in enumerate(((got_out, corner_out), (got_back, corner_back))):
        low = sends_up(side == 1)
        there = jnp.where(low, has_prev("space"), has_next("space"))

        def at(q, low=low):
            return jnp.where(low, q, nx - 1 - q)

        def place(name, q, j, got=got, corner=corner, low=low, at=at):
            if name in own:
                if q >= 0:
                    return (strips[name], at(q), 0) if j == n else (own[name], at(q), ROWS * j)
                if name == "r":
                    return got, 4, ROWS * j
                if j == n:
                    return corner, corner_at[name], 0
                return got, got_at[name] + jnp.where(low, 2 + q, -1 - q), ROWS * j
            if q <= 0:
                return made[name], 1 + q, ROWS * j
            i = jnp.where(low, q, nx - 2 - q) if name == "cx" else at(q)
            return made_place(middles, ends, n, name, i, j)

        slab = Slab(place, lambda name, q: (rings[name], q % 2), ny, nz, mask)
        keep = jnp.broadcast_to(jnp.where(there, 1, 0), (ROWS, LANES)) == 1
        run(slab.load(-1, range(n + 1), TURNED1), slab.load(0, range(n + 1), TURNED1))
        run(slab.load(1, range(n + 1), TURNED2))
        run(slab.first(-1, range(n), keep=keep))
        run(slab.first(0, range(n + 1)))
        run(slab.load(0, range(n + 1), TURNED2))
        for q in (0, 1):
            run(slab.second(q, out, 2 * side + q))
            c = pltpu.make_async_copy(out.at[2 * side + q], out_hbm.at[at(q)], sems.at[2 * side + q])
            c.start()
            writes.append(c)
    for c in writes:
        c.wait()


def outer(own, strips, got, corners, middles, ends, out):
    nx, ny, nz = own[0].shape
    args = (*own, *strips, *got, *corners, *middles, *ends)
    return pl.pallas_call(
        outer_kernel,
        out_shape=jax.ShapeDtypeStruct((nx, ny, nz), F32),
        in_specs=[VMEM] * len(args) + [HBM],
        out_specs=HBM,
        input_output_aliases={len(args): 0},
        scratch_shapes=[pltpu.VMEM((2, ny + ROWS, nz), F32)] * len(MADE)
        + [pltpu.VMEM(turned_shape(2, ny, nz), F32)] * 4
        + [pltpu.VMEM((4, ny, nz), F32), pltpu.SemaphoreType.DMA((4,))],
        compiler_params=pltpu.CompilerParams(vmem_limit_bytes=6 * 2**20),
        name="outer",
    )(*args, out)


def shards(residual, mobility, initial_guess):
    own = (initial_guess, mobility, residual)
    *rows, plane_out, plane_back = send(*(pltpu.with_memory_space_constraint(v, pltpu.HBM) for v in own))
    got = [along_space(v, back) for v, back in ((plane_out, False), (plane_back, True))]
    rows = [along_member(v, back) for v, back in zip(rows, (False, True))]
    middles = middle(own)
    *strips, corner_out, corner_back = halo(*rows, residual.shape[0], middles[-1])
    corners = [along_space(v, back) for v, back in ((corner_out, False), (corner_back, True))]
    out, *ends = inner(own, strips, middles)
    return outer(own, strips, got, corners, middles, ends, out)


def solution(mesh):
    placed = P("space", "member", None)
    return jax.shard_map(shards, mesh=mesh, in_specs=(placed,) * 3, out_specs=placed, check_vma=False)
```

```python
import math

import jax
import jax.numpy as jnp
from jax import lax
from jax.experimental import pallas as pl
from jax.experimental.pallas import tpu as pltpu
from jax.sharding import PartitionSpec as P

sweep_weights = tuple((1.0 / (1.15 + 0.85 * math.cos(math.pi * (2 * j - 1) / 4.0)) for j in (1, 2)))

LANES = 128
ROWS = 8
VMEM = pl.BlockSpec(memory_space=pltpu.VMEM)
HBM = pl.BlockSpec(memory_space=pltpu.HBM)
F32 = jnp.float32


def lane_slices(nz):
    return [slice(k * LANES, (k + 1) * LANES) for k in range(nz // LANES)]


def iotas():
    row = lax.broadcasted_iota(jnp.int32, (ROWS, LANES), 0)
    lane = lax.broadcasted_iota(jnp.int32, (ROWS, LANES), 1)
    return row, lane


def next_lanes(vals, last_lane):
    turned = [pltpu.roll(v, LANES - 1, 1) for v in vals]
    return [jnp.where(last_lane, b, a) for a, b in zip(turned, turned[1:] + [0.0])]


def prev_lanes(vals, first_lane):
    turned = [pltpu.roll(v, 1, 1) for v in vals]
    return [jnp.where(first_lane, b, a) for a, b in zip(turned, [0.0] + turned[:-1])]


class Slab:
    def __init__(self, place, turning, ny, nz, row_ok):
        self.place, self.turning = place, turning
        self.strips = ny // ROWS
        self.tiles = lane_slices(nz)
        self.row_ok = row_ok
        _, lane = iotas()
        self.first_lane, self.last_lane = lane == 0, lane == LANES - 1

    def get(self, name, i, j):
        ref, at, row = self.place(name, i, j)
        return [ref[at, row : row + ROWS, s] for s in self.tiles]

    def put(self, name, i, j, vals):
        ref, at, row = self.place(name, i, j)
        for s, v in zip(self.tiles, vals):
            ref[at, row : row + ROWS, s] = v

    def load(self, i, strips, names):
        for j in strips:
            for name in names:
                ref, at = self.turning(name, i)
                vals = self.get(name, i, j)
                for row in (0, ROWS * (j + 1)) if j == self.strips else (ROWS * (j + 1),):
                    for k, v in enumerate(vals):
                        ref[at, k, row : row + ROWS, :] = v
            yield

    def shifted(self, name, i, j, by=0):
        ref, at = self.turning(name, i)
        if j == self.strips:
            row = {0: 0, 1: 1, -1: ROWS * (j + 1) - 1}[by]
        else:
            row = ROWS * (j + 1) + by
        return [ref[at, k, row : row + ROWS, :] for k in range(len(self.tiles))]

    def first(self, i, strips, keep=None, e_before=True):
        w = sweep_weights[0]
        n = self.strips
        strips = list(strips)

        def ahead(j):
            e, m = self.shifted("e", i, j), self.shifted("m", i, j)
            return (
                e,
                m,
                next_lanes(e, self.last_lane),
                prev_lanes(e, self.first_lane),
                next_lanes(m, self.last_lane),
                prev_lanes(m, self.first_lane),
            )

        here = ahead(strips[0])
        for j, after in zip(strips, strips[1:] + [None]):
            there = None if after is None else ahead(after)
            e, m, e_zp, e_zm, m_zp, m_zm = here
            e_up, e_dn = self.shifted("e", i, j, 1), self.shifted("e", i, j, -1)
            m_up, m_dn = self.shifted("m", i, j, 1), self.shifted("m", i, j, -1)
            e_xp, e_xm = self.get("e", i + 1, j), self.get("e", i - 1, j) if e_before else None
            m_xp, m_xm = self.get("m", i + 1, j), self.get("m", i - 1, j)
            r = self.get("r", i, j)
            made = []
            for k in range(len(self.tiles)):
                cx, cxm = m[k] + m_xp[k], m[k] + m_xm[k]
                cy, cy_dn = m[k] + m_up[k], m[k] + m_dn[k]
                cz, cz_dn = m[k] + m_zp[k], m[k] + m_zm[k]
                t = ((cx + cxm) + (cy + cy_dn)) + (cz + cz_dn)
                num_x = cx * e_xp[k] + cxm * e_xm[k] if e_before else cx * e_xp[k]
                num = (num_x + (cy * e_up[k] + cy_dn * e_dn[k])) + ((cz * e_zp[k] + cz_dn * e_zm[k]) + (r[k] + r[k]))
                rt = 1.0 / t
                e1 = (1.0 - w) * e[k] + (w * rt) * num
                if j == n:
                    e1 = jnp.where(self.row_ok, e1, 0.0)
                if keep is not None:
                    e1 = jnp.where(keep, e1, 0.0)
                made.append((cx, cy, cz, rt, e1))
            cx, cy, cz, rt, e1 = zip(*made)
            self.put("cy", i, j, cy)
            self.put("e1", i, j, e1)
            if j < n:
                self.put("cx", i, j, cx)
                self.put("cz", i, j, cz)
                self.put("rt", i, j, rt)
            here = there
            yield

    def second(self, i, out, o):
        w = sweep_weights[1]

        def ahead(j):
            e, cz = self.shifted("e1", i, j), self.get("cz", i, j)
            return e, cz, next_lanes(e, self.last_lane), prev_lanes([a * b for a, b in zip(cz, e)], self.first_lane)

        here = ahead(0)
        for j in range(self.strips):
            there = ahead(j + 1) if j < self.strips - 1 else None
            e, cz, e_zp, h_dn = here
            e_up, e_dn = self.shifted("e1", i, j, 1), self.shifted("e1", i, j, -1)
            cy, cy_dn = self.shifted("cy", i, j), self.shifted("cy", i, j, -1)
            e_xp, e_xm = self.get("e1", i + 1, j), self.get("e1", i - 1, j)
            cx, cxm = self.get("cx", i, j), self.get("cx", i - 1, j)
            rt = self.get("rt", i, j)
            r = self.get("r", i, j)
            outs = []
            for k in range(len(self.tiles)):
                num = ((cx[k] * e_xp[k] + cxm[k] * e_xm[k]) + (cy[k] * e_up[k] + cy_dn[k] * e_dn[k])) + (
                    (cz[k] * e_zp[k] + h_dn[k]) + (r[k] + r[k])
                )
                outs.append((1.0 - w) * e[k] + (w * rt[k]) * num)
            for s, v in zip(self.tiles, outs):
                out[o, ROWS * j : ROWS * (j + 1), s] = v
            here = there
            yield


def run(*passes):
    passes = list(passes)
    while passes:
        passes = [p for p in passes if next(p, StopIteration) is not StopIteration]


RING = 6
TURNED1, TURNED2 = ("e", "m"), ("e1", "cy")
MADE = ("e1", "cy", "cx", "cz", "rt")


def turned_shape(planes, ny, nz):
    return (planes, nz // LANES, ny + 2 * ROWS, LANES)


class Plane:
    def __init__(self, number, slot):
        self.number, self.slot = number, slot

    def __add__(self, by):
        return Plane(self.number + by, (self.slot + by) % RING)

    def __sub__(self, by):
        return self + -by

    def load(self, by, last):
        return Plane(jnp.minimum(self.number + by, last), (self.slot + by) % RING)


def number(i):
    return i.number if isinstance(i, Plane) else i


def along_space(x, back):
    ns, nm = lax.axis_size("space"), lax.axis_size("member")
    hops = []
    for m in range(nm):
        step = 1 if m % 2 == 0 else -1
        for i in range(ns):
            to = (i + step, m) if 0 <= i + step < ns else (i, m + step)
            hops.append((i * nm + m, to[0] * nm + to[1]))
    return lax.ppermute(x, ("space", "member"), [(b, a) for a, b in hops] if back else hops)


def along_member(x, back):
    n = lax.axis_size("member")
    return lax.ppermute(x, "member", [((i + 1) % n, i) if back else (i, (i + 1) % n) for i in range(n)])


def sends_up(back):
    even = lax.rem(lax.axis_index("member"), 2) == 0
    return jnp.logical_not(even) if back else even


def has_next(axis):
    return lax.axis_index(axis) < lax.axis_size(axis) - 1


def has_prev(axis):
    return lax.axis_index(axis) > 0


def row_mask():
    row, _ = iotas()
    after, before = jnp.where(has_next("member"), 1, 0), jnp.where(has_prev("member"), 1, 0)
    return jnp.where(row < ROWS // 2, after, before) == 1


def with_behind(e_behind, m_behind, m, r):
    return r + (0.5 * e_behind) * (m + m_behind)


def send_kernel(e, m, r, to_next, to_prev, plane_out, plane_back, top, bottom, planes, sems, plane_sems):
    nx, ny, nz = e.shape
    groups = nx // ROWS
    reads = []
    for k, src in enumerate((e, m, r)):
        for dst, at in ((top, 0), (bottom, ny - ROWS)):
            rows = 1 if k == 2 else 2
            first = 0 if at == 0 else ROWS - rows
            here, there = src.at[:, at + first : at + first + rows], dst.at[k, :, first : first + rows]
            reads.append(pltpu.make_async_copy(here, there, sems.at[len(reads)]))
    for c in reads:
        c.start()
    reads2 = []
    for side, (dst, back) in enumerate(((plane_out, False), (plane_back, True))):
        up = sends_up(back)
        end, behind = jnp.where(up, nx - 1, 0), jnp.where(up, nx - 2, 1)
        for src, at, to in (
            (e, end, dst.at[0]),
            (m, end, dst.at[1]),
            (m, behind, dst.at[2]),
            (e, behind, planes.at[2 * side]),
            (r, end, planes.at[2 * side + 1]),
        ):
            reads2.append(pltpu.make_async_copy(src.at[at], to, plane_sems.at[len(reads2)]))
    for c in reads2:
        c.start()
    for c in reads:
        c.wait()
    next_ok, prev_ok = has_next("member"), has_prev("member")
    for dst, strips, end, behind, ok in (
        (to_next, bottom, ROWS - 1, ROWS - 2, next_ok),
        (to_prev, top, 0, 1, prev_ok),
    ):
        for g in range(groups):
            at = slice(ROWS * g, ROWS * (g + 1))
            e_behind, m_behind = strips[0, at, behind, :], strips[1, at, behind, :]
            e_end, m_end, r_end = (strips[k, at, end, :] for k in range(3))
            for n, v in enumerate((e_end, m_end, m_behind, with_behind(e_behind, m_behind, m_end, r_end))):
                dst[groups * n + g] = jnp.where(ok, v, 0.0)
    for c in reads2:
        c.wait()
    for side, (dst, back) in enumerate(((plane_out, False), (plane_back, True))):

        @pl.loop(0, ny // ROWS)
        def _(j, side=side, dst=dst):
            at = pl.ds(pl.multiple_of(j * ROWS, ROWS), ROWS)
            dst[3, at, :] = with_behind(planes[2 * side, at, :], dst[2, at, :], dst[1, at, :], planes[2 * side + 1, at, :])

        @pl.when(jnp.logical_not(jnp.where(sends_up(back), has_next("space"), has_prev("space"))))
        def _(dst=dst):
            dst[...] = jnp.zeros_like(dst)


def send(e, m, r):
    nx, ny, nz = e.shape
    rows = jax.ShapeDtypeStruct((4 * (nx // ROWS), ROWS, nz), F32)
    planes = jax.ShapeDtypeStruct((4, ny, nz), F32)
    strips = pltpu.VMEM((3, nx, ROWS, nz), F32)
    return pl.pallas_call(
        send_kernel,
        out_shape=[rows, rows, planes, planes],
        in_specs=[HBM] * 3,
        out_specs=[VMEM] * 4,
        scratch_shapes=[strips, strips, pltpu.VMEM((4, ny, nz), F32)]
        + [pltpu.SemaphoreType.DMA((6,)), pltpu.SemaphoreType.DMA((10,))],
        compiler_params=pltpu.CompilerParams(vmem_limit_bytes=8 * 2**20),
        name="send",
    )(e, m, r)


def halo_kernel(from_prev, from_next, _, eh, mh, rh, corner_out, corner_back):
    nx, _, nz = eh.shape
    groups = nx // ROWS
    for ref in (eh, mh, rh):
        ref[...] = jnp.zeros_like(ref)
    for n, (ref, below, above) in enumerate(((eh, 1, 0), (mh, 1, 0), (mh, 2, 1), (rh, 1, 0))):
        for g in range(groups):
            at = slice(ROWS * g, ROWS * (g + 1))
            ref[at, ROWS - below, :] = from_prev[groups * n + g]
            ref[at, above, :] = from_next[groups * n + g]
    for dst, back in ((corner_out, False), (corner_back, True)):
        up = sends_up(back)
        ok = jnp.where(up, has_next("space"), has_prev("space"))
        at = jnp.where(up, nx - 1, 0)
        dst[0] = jnp.where(ok, eh[at], 0.0)
        dst[1] = jnp.where(ok, mh[at], 0.0)


def halo(from_prev, from_next, nx, after):
    nz = from_prev.shape[2]
    strip = jax.ShapeDtypeStruct((nx, ROWS, nz), F32)
    corner = jax.ShapeDtypeStruct((2, ROWS, nz), F32)
    return pl.pallas_call(
        halo_kernel,
        out_shape=[strip] * 3 + [corner] * 2,
        in_specs=[VMEM] * 2 + [pl.BlockSpec(memory_space=pl.ANY)],
        out_specs=[VMEM] * 5,
        compiler_params=pltpu.CompilerParams(vmem_limit_bytes=2 * 2**20),
        name="halo",
    )(from_prev, from_next, after)


def middle_kernel(e, m, r, *rest):
    nx, ny, nz = e.shape
    arrays = dict(zip(("e", "m", "r") + MADE, (e, m, r) + rest))
    rings = dict(zip(TURNED1, rest[len(MADE) :]))
    slab = Slab(
        lambda name, i, j: (arrays[name], number(i), ROWS * j), lambda name, i: (rings[name], i.slot), ny, nz, None
    )
    strips = range(slab.strips)
    for k in range(RING // 2):
        run(slab.load(Plane(1 + k, k), strips, TURNED1))

    @pl.loop(0, (nx - 2) // RING)
    def _(t):
        for k in range(RING):
            i = Plane(1 + RING * t + k, k)
            run(slab.first(i, strips[1:-1]), slab.load(i.load(RING // 2, nx - 2), strips, TURNED1))


def middle(own):
    nx, ny, nz = own[0].shape
    return pl.pallas_call(
        middle_kernel,
        out_shape=[jax.ShapeDtypeStruct((nx, ny, nz), F32)] * len(MADE),
        in_specs=[VMEM] * 3,
        out_specs=[VMEM] * len(MADE),
        scratch_shapes=[pltpu.VMEM(turned_shape(RING, ny, nz), F32)] * 2,
        compiler_params=pltpu.CompilerParams(vmem_limit_bytes=4 * 2**20),
        cost_estimate=pl.CostEstimate(flops=40 * nx * ny * nz, bytes_accessed=16 * nx * ny * nz, transcendentals=0),
        name="middle",
    )(*own)


def made_place(middles, ends, n, name, i, end, j):
    if 0 < j < n - 1:
        return middles[name], i, ROWS * j
    return ends[name], end, ROWS * {0: 0, n - 1: 1, n: 2}[j]


def inner_kernel(e, m, r, eh, mh, rh, *rest):
    nx, ny, nz = e.shape
    n = ny // ROWS
    own = {"e": (e, eh), "m": (m, mh), "r": (r, rh)}
    count = len(MADE)
    middles, rest = dict(zip(MADE, rest)), rest[count:]
    out_hbm, handed, rest = rest[0], dict(zip(MADE, rest[1:])), rest[1 + count :]
    ends, rest = dict(zip(MADE, rest)), rest[count:]
    rings, (out, sems) = dict(zip(TURNED1 + TURNED2, rest)), rest[4:]

    def place(name, i, j):
        if name in own:
            ref, strip = own[name]
            return (strip, number(i), 0) if j == n else (ref, number(i), ROWS * j)
        return made_place(middles, ends, n, name, number(i), i.slot, j)

    slab = Slab(place, lambda name, i: (rings[name], i.slot), ny, nz, row_mask())
    around = [0, 1, n - 2, n - 1, n]
    ahead, behind = RING // 2, 3

    def out_copy(i):
        return pltpu.make_async_copy(out.at[i], out_hbm.at[i], sems.at[i])

    def second(i):
        return slab.second(i, out, number(i))

    def first(i):
        return [
            slab.first(i, [0, n - 1, n]),
            slab.load(i.load(ahead, nx - 2), around, TURNED1),
            slab.load(i - 1, range(n + 1), TURNED2),
        ]

    def hand(k, slot):
        for name in MADE:
            handed[name][k] = ends[name][slot]

    for k in range(ahead):
        run(slab.load(Plane(1 + k, k), around, TURNED1))
    for k in range(RING):
        i = Plane(1 + k, k)
        if i.number < 2 + behind:
            run(*first(i)[: 2 if k == 0 else 3])
        else:
            run(second(i - behind), *first(i))
            out_copy(i.number - behind).start()
    hand(0, 0)
    hand(1, 1)

    @pl.loop(1, (nx - 2) // RING)
    def _(t):
        for k in range(RING):
            i = Plane(1 + RING * t + k, k)
            run(second(i - behind), *first(i))
            out_copy(i.number - behind).start()

    hand(2, (nx - 4) % RING)
    hand(3, (nx - 3) % RING)
    for i in (nx - 4, nx - 3):
        run(second(Plane(i, (i - 1) % RING)))
        out_copy(i).start()

    @pl.loop(2, nx - 2)
    def _(i):
        out_copy(i).wait()


def inner(own, strips, middles):
    nx, ny, nz = own[0].shape
    args = (*own, *strips, *middles)
    return pl.pallas_call(
        inner_kernel,
        out_shape=[jax.ShapeDtypeStruct((nx, ny, nz), F32)] + [jax.ShapeDtypeStruct((4, 3 * ROWS, nz), F32)] * len(MADE),
        in_specs=[VMEM] * len(args),
        out_specs=[HBM] + [VMEM] * len(MADE),
        scratch_shapes=[pltpu.VMEM((RING, 3 * ROWS, nz), F32)] * len(MADE)
        + [pltpu.VMEM(turned_shape(RING, ny, nz), F32)] * 4
        + [pltpu.VMEM((nx, ny, nz), F32), pltpu.SemaphoreType.DMA((nx,))],
        compiler_params=pltpu.CompilerParams(vmem_limit_bytes=11 * 2**20),
        cost_estimate=pl.CostEstimate(flops=40 * nx * ny * nz, bytes_accessed=16 * nx * ny * nz, transcendentals=0),
        name="inner",
    )(*args)


def outer_kernel(e, m, r, eh, mh, rh, got_out, got_back, corner_out, corner_back, *rest):
    nx, ny, nz = e.shape
    n = ny // ROWS
    count = len(MADE)
    middles, ends, rest = dict(zip(MADE, rest)), dict(zip(MADE, rest[count:])), rest[2 * count + 1 :]
    out_hbm, made, rest = rest[0], dict(zip(MADE, rest[1:])), rest[1 + count :]
    rings, (out, sems) = dict(zip(TURNED1 + TURNED2, rest)), rest[4:]
    own = {"e": e, "m": m, "r": r}
    strips = {"e": eh, "m": mh, "r": rh}
    got_at = {("e", -1): 0, ("m", -1): 1, ("m", -2): 2, ("r", -1): 3}
    corner_at = {"e": 0, "m": 1}
    mask = row_mask()
    writes = []
    for side, (got, corner) in enumerate(((got_out, corner_out), (got_back, corner_back))):
        low = sends_up(side == 1)
        there = jnp.where(low, has_prev("space"), has_next("space"))

        def at(q, low=low):
            return jnp.where(low, q, nx - 1 - q)

        def place(name, q, j, got=got, corner=corner, low=low, at=at):
            if name in own:
                if q >= 0:
                    return (strips[name], at(q), 0) if j == n else (own[name], at(q), ROWS * j)
                if j == n:
                    return corner, corner_at[name], 0
                return got, got_at[name, q], ROWS * j
            if q <= 0:
                return made[name], 1 + q, ROWS * j
            i = jnp.where(low, q, nx - 2 - q) if name == "cx" else at(q)
            end = jnp.where(low, q - 1, 3 - q if name == "cx" else 4 - q)
            return made_place(middles, ends, n, name, i, end, j)

        slab = Slab(place, lambda name, q: (rings[name], q % 2), ny, nz, mask)
        keep = jnp.broadcast_to(jnp.where(there, 1, 0), (ROWS, LANES)) == 1
        run(slab.load(-1, range(n + 1), TURNED1), slab.load(0, range(n + 1), TURNED1))
        run(slab.load(1, range(n + 1), TURNED2))
        run(slab.first(-1, range(n), keep=keep, e_before=False))
        run(slab.first(0, range(n + 1)))
        run(slab.load(0, range(n + 1), TURNED2))
        for q in (0, 1):
            run(slab.second(q, out, 2 * side + q))
            c = pltpu.make_async_copy(out.at[2 * side + q], out_hbm.at[at(q)], sems.at[2 * side + q])
            c.start()
            writes.append(c)
    for c in writes:
        c.wait()


def outer(own, strips, got, corners, middles, ends, out):
    nx, ny, nz = own[0].shape
    args = (*own, *strips, *got, *corners, *middles, *ends)
    return pl.pallas_call(
        outer_kernel,
        out_shape=jax.ShapeDtypeStruct((nx, ny, nz), F32),
        in_specs=[VMEM] * len(args) + [HBM],
        out_specs=HBM,
        input_output_aliases={len(args): 0},
        scratch_shapes=[pltpu.VMEM((2, ny + ROWS, nz), F32)] * len(MADE)
        + [pltpu.VMEM(turned_shape(2, ny, nz), F32)] * 4
        + [pltpu.VMEM((4, ny, nz), F32), pltpu.SemaphoreType.DMA((4,))],
        compiler_params=pltpu.CompilerParams(vmem_limit_bytes=6 * 2**20),
        name="outer",
    )(*args, out)


def shards(residual, mobility, initial_guess):
    own = (initial_guess, mobility, residual)
    *rows, plane_out, plane_back = send(*(pltpu.with_memory_space_constraint(v, pltpu.HBM) for v in own))
    got = [along_space(v, back) for v, back in ((plane_out, False), (plane_back, True))]
    rows = [along_member(v, back) for v, back in zip(rows, (False, True))]
    middles = middle(own)
    *strips, corner_out, corner_back = halo(*rows, residual.shape[0], middles[-1])
    corners = [along_space(v, back) for v, back in ((corner_out, False), (corner_back, True))]
    out, *ends = inner(own, strips, middles)
    return outer(own, strips, got, corners, middles, ends, out)


def solution(mesh):
    placed = P("space", "member", None)
    return jax.shard_map(shards, mesh=mesh, in_specs=(placed,) * 3, out_specs=placed, check_vma=False)
```

```python
import math

import jax
import jax.numpy as jnp
from jax import lax
from jax.experimental import pallas as pl
from jax.experimental.pallas import tpu as pltpu
from jax.sharding import PartitionSpec as P

sweep_weights = tuple((1.0 / (1.15 + 0.85 * math.cos(math.pi * (2 * j - 1) / 4.0)) for j in (1, 2)))

LANES = 128
ROWS = 8
VMEM = pl.BlockSpec(memory_space=pltpu.VMEM)
HBM = pl.BlockSpec(memory_space=pltpu.HBM)
F32 = jnp.float32


def lane_slices(nz):
    return [slice(k * LANES, (k + 1) * LANES) for k in range(nz // LANES)]


def iotas():
    row = lax.broadcasted_iota(jnp.int32, (ROWS, LANES), 0)
    lane = lax.broadcasted_iota(jnp.int32, (ROWS, LANES), 1)
    return row, lane


def next_lanes(vals, last_lane):
    turned = [pltpu.roll(v, LANES - 1, 1) for v in vals]
    return [jnp.where(last_lane, b, a) for a, b in zip(turned, turned[1:] + [0.0])]


def prev_lanes(vals, first_lane):
    turned = [pltpu.roll(v, 1, 1) for v in vals]
    return [jnp.where(first_lane, b, a) for a, b in zip(turned, [0.0] + turned[:-1])]


class Slab:
    def __init__(self, place, turning, ny, nz, row_ok):
        self.place, self.turning = place, turning
        self.strips = ny // ROWS
        self.tiles = lane_slices(nz)
        self.row_ok = row_ok
        _, lane = iotas()
        self.first_lane, self.last_lane = lane == 0, lane == LANES - 1

    def get(self, name, i, j):
        ref, at, row = self.place(name, i, j)
        return [ref[at, row : row + ROWS, s] for s in self.tiles]

    def put(self, name, i, j, vals):
        ref, at, row = self.place(name, i, j)
        for s, v in zip(self.tiles, vals):
            ref[at, row : row + ROWS, s] = v

    def load(self, i, strips, names):
        for j in strips:
            for name in names:
                ref, at = self.turning(name, i)
                vals = self.get(name, i, j)
                for row in (0, ROWS * (j + 1)) if j == self.strips else (ROWS * (j + 1),):
                    for k, v in enumerate(vals):
                        ref[at, k, row : row + ROWS, :] = v
            yield

    def shifted(self, name, i, j, by=0):
        ref, at = self.turning(name, i)
        if j == self.strips:
            row = {0: 0, 1: 1, -1: ROWS * (j + 1) - 1}[by]
        else:
            row = ROWS * (j + 1) + by
        return [ref[at, k, row : row + ROWS, :] for k in range(len(self.tiles))]

    def first(self, i, strips, keep=None, e_before=True):
        w = sweep_weights[0]
        n = self.strips
        strips = list(strips)

        def ahead(j):
            e, m = self.shifted("e", i, j), self.shifted("m", i, j)
            return (
                e,
                m,
                next_lanes(e, self.last_lane),
                prev_lanes(e, self.first_lane),
                next_lanes(m, self.last_lane),
                prev_lanes(m, self.first_lane),
            )

        here = ahead(strips[0])
        for j, after in zip(strips, strips[1:] + [None]):
            there = None if after is None else ahead(after)
            e, m, e_zp, e_zm, m_zp, m_zm = here
            e_up, e_dn = self.shifted("e", i, j, 1), self.shifted("e", i, j, -1)
            m_up, m_dn = self.shifted("m", i, j, 1), self.shifted("m", i, j, -1)
            e_xp, e_xm = self.get("e", i + 1, j), self.get("e", i - 1, j) if e_before else None
            m_xp, m_xm = self.get("m", i + 1, j), self.get("m", i - 1, j)
            r = self.get("r", i, j)
            made = []
            for k in range(len(self.tiles)):
                cx, cxm = m[k] + m_xp[k], m[k] + m_xm[k]
                cy, cy_dn = m[k] + m_up[k], m[k] + m_dn[k]
                cz, cz_dn = m[k] + m_zp[k], m[k] + m_zm[k]
                t = ((cx + cxm) + (cy + cy_dn)) + (cz + cz_dn)
                num_x = cx * e_xp[k] + cxm * e_xm[k] if e_before else cx * e_xp[k]
                num = (num_x + (cy * e_up[k] + cy_dn * e_dn[k])) + ((cz * e_zp[k] + cz_dn * e_zm[k]) + (r[k] + r[k]))
                rt = 1.0 / t
                e1 = (1.0 - w) * e[k] + (w * rt) * num
                if j == n:
                    e1 = jnp.where(self.row_ok, e1, 0.0)
                if keep is not None:
                    e1 = jnp.where(keep, e1, 0.0)
                made.append((cx, cy, cz, rt, e1))
            cx, cy, cz, rt, e1 = zip(*made)
            self.put("cy", i, j, cy)
            self.put("e1", i, j, e1)
            if j < n:
                self.put("cx", i, j, cx)
                self.put("cz", i, j, cz)
                self.put("rt", i, j, rt)
            here = there
            yield

    def second(self, i, out, o):
        w = sweep_weights[1]

        def ahead(j):
            e, cz = self.shifted("e1", i, j), self.get("cz", i, j)
            return e, cz, next_lanes(e, self.last_lane), prev_lanes([a * b for a, b in zip(cz, e)], self.first_lane)

        here = ahead(0)
        for j in range(self.strips):
            there = ahead(j + 1) if j < self.strips - 1 else None
            e, cz, e_zp, h_dn = here
            e_up, e_dn = self.shifted("e1", i, j, 1), self.shifted("e1", i, j, -1)
            cy, cy_dn = self.shifted("cy", i, j), self.shifted("cy", i, j, -1)
            e_xp, e_xm = self.get("e1", i + 1, j), self.get("e1", i - 1, j)
            cx, cxm = self.get("cx", i, j), self.get("cx", i - 1, j)
            rt = self.get("rt", i, j)
            r = self.get("r", i, j)
            outs = []
            for k in range(len(self.tiles)):
                num = ((cx[k] * e_xp[k] + cxm[k] * e_xm[k]) + (cy[k] * e_up[k] + cy_dn[k] * e_dn[k])) + (
                    (cz[k] * e_zp[k] + h_dn[k]) + (r[k] + r[k])
                )
                outs.append((1.0 - w) * e[k] + (w * rt[k]) * num)
            for s, v in zip(self.tiles, outs):
                out[o, ROWS * j : ROWS * (j + 1), s] = v
            here = there
            yield


def run(*passes):
    passes = list(passes)
    while passes:
        passes = [p for p in passes if next(p, StopIteration) is not StopIteration]


RING = 6
TURNED1, TURNED2 = ("e", "m"), ("e1", "cy")
MADE = ("e1", "cy", "cx", "cz", "rt")


def turned_shape(planes, ny, nz):
    return (planes, nz // LANES, ny + 2 * ROWS, LANES)


class Plane:
    def __init__(self, number, slot):
        self.number, self.slot = number, slot

    def __add__(self, by):
        return Plane(self.number + by, (self.slot + by) % RING)

    def __sub__(self, by):
        return self + -by

    def load(self, by, last):
        return Plane(jnp.minimum(self.number + by, last), (self.slot + by) % RING)


def number(i):
    return i.number if isinstance(i, Plane) else i


def along_space(x, back):
    ns, nm = lax.axis_size("space"), lax.axis_size("member")
    hops = []
    for m in range(nm):
        step = 1 if m % 2 == 0 else -1
        for i in range(ns):
            to = (i + step, m) if 0 <= i + step < ns else (i, m + step)
            hops.append((i * nm + m, to[0] * nm + to[1]))
    return lax.ppermute(x, ("space", "member"), [(b, a) for a, b in hops] if back else hops)


def along_member(x, back):
    n = lax.axis_size("member")
    return lax.ppermute(x, "member", [((i + 1) % n, i) if back else (i, (i + 1) % n) for i in range(n)])


def sends_up(back):
    even = lax.rem(lax.axis_index("member"), 2) == 0
    return jnp.logical_not(even) if back else even


def has_next(axis):
    return lax.axis_index(axis) < lax.axis_size(axis) - 1


def has_prev(axis):
    return lax.axis_index(axis) > 0


def row_mask():
    row, _ = iotas()
    after, before = jnp.where(has_next("member"), 1, 0), jnp.where(has_prev("member"), 1, 0)
    return jnp.where(row < ROWS // 2, after, before) == 1


def with_behind(e_behind, m_behind, m, r):
    return r + (0.5 * e_behind) * (m + m_behind)


def send_kernel(e, m, r, to_next, to_prev, plane_out, plane_back, top, bottom, planes, sems, plane_sems):
    nx, ny, nz = e.shape
    groups = nx // ROWS
    reads = []
    for k, src in enumerate((e, m, r)):
        for dst, at in ((top, 0), (bottom, ny - ROWS)):
            rows = 1 if k == 2 else 2
            first = 0 if at == 0 else ROWS - rows
            here, there = src.at[:, at + first : at + first + rows], dst.at[k, :, first : first + rows]
            reads.append(pltpu.make_async_copy(here, there, sems.at[len(reads)]))
    for c in reads:
        c.start()
    reads2 = []
    for side, (dst, back) in enumerate(((plane_out, False), (plane_back, True))):
        up = sends_up(back)
        end, behind = jnp.where(up, nx - 1, 0), jnp.where(up, nx - 2, 1)
        for src, at, to in (
            (e, end, dst.at[0]),
            (m, end, dst.at[1]),
            (m, behind, dst.at[2]),
            (e, behind, planes.at[2 * side]),
            (r, end, planes.at[2 * side + 1]),
        ):
            reads2.append(pltpu.make_async_copy(src.at[at], to, plane_sems.at[len(reads2)]))
    for c in reads2:
        c.start()
    for c in reads:
        c.wait()
    next_ok, prev_ok = has_next("member"), has_prev("member")
    for dst, strips, end, behind, ok in (
        (to_next, bottom, ROWS - 1, ROWS - 2, next_ok),
        (to_prev, top, 0, 1, prev_ok),
    ):
        for g in range(groups):
            at = slice(ROWS * g, ROWS * (g + 1))
            e_behind, m_behind = strips[0, at, behind, :], strips[1, at, behind, :]
            e_end, m_end, r_end = (strips[k, at, end, :] for k in range(3))
            for n, v in enumerate((e_end, m_end, m_behind, with_behind(e_behind, m_behind, m_end, r_end))):
                dst[groups * n + g] = jnp.where(ok, v, 0.0)
    for c in reads2:
        c.wait()
    for side, (dst, back) in enumerate(((plane_out, False), (plane_back, True))):

        @pl.loop(0, ny // ROWS)
        def _(j, side=side, dst=dst):
            at = pl.ds(pl.multiple_of(j * ROWS, ROWS), ROWS)
            dst[3, at, :] = with_behind(planes[2 * side, at, :], dst[2, at, :], dst[1, at, :], planes[2 * side + 1, at, :])

        @pl.when(jnp.logical_not(jnp.where(sends_up(back), has_next("space"), has_prev("space"))))
        def _(dst=dst):
            dst[...] = jnp.zeros_like(dst)


def send(e, m, r):
    nx, ny, nz = e.shape
    rows = jax.ShapeDtypeStruct((4 * (nx // ROWS), ROWS, nz), F32)
    planes = jax.ShapeDtypeStruct((4, ny, nz), F32)
    strips = pltpu.VMEM((3, nx, ROWS, nz), F32)
    return pl.pallas_call(
        send_kernel,
        out_shape=[rows, rows, planes, planes],
        in_specs=[HBM] * 3,
        out_specs=[VMEM] * 4,
        scratch_shapes=[strips, strips, pltpu.VMEM((4, ny, nz), F32)]
        + [pltpu.SemaphoreType.DMA((6,)), pltpu.SemaphoreType.DMA((10,))],
        compiler_params=pltpu.CompilerParams(vmem_limit_bytes=8 * 2**20),
        name="send",
    )(e, m, r)


def halo_kernel(from_prev, from_next, _, eh, mh, rh, corner_out, corner_back):
    nx, _, nz = eh.shape
    groups = nx // ROWS
    for ref in (eh, mh, rh):
        ref[...] = jnp.zeros_like(ref)
    for n, (ref, below, above) in enumerate(((eh, 1, 0), (mh, 1, 0), (mh, 2, 1), (rh, 1, 0))):
        for g in range(groups):
            at = slice(ROWS * g, ROWS * (g + 1))
            ref[at, ROWS - below, :] = from_prev[groups * n + g]
            ref[at, above, :] = from_next[groups * n + g]
    for dst, back in ((corner_out, False), (corner_back, True)):
        up = sends_up(back)
        ok = jnp.where(up, has_next("space"), has_prev("space"))
        at = jnp.where(up, nx - 1, 0)
        dst[0] = jnp.where(ok, eh[at], 0.0)
        dst[1] = jnp.where(ok, mh[at], 0.0)


def halo(from_prev, from_next, nx, after):
    nz = from_prev.shape[2]
    strip = jax.ShapeDtypeStruct((nx, ROWS, nz), F32)
    corner = jax.ShapeDtypeStruct((2, ROWS, nz), F32)
    return pl.pallas_call(
        halo_kernel,
        out_shape=[strip] * 3 + [corner] * 2,
        in_specs=[VMEM] * 2 + [pl.BlockSpec(memory_space=pl.ANY)],
        out_specs=[VMEM] * 5,
        compiler_params=pltpu.CompilerParams(vmem_limit_bytes=2 * 2**20),
        name="halo",
    )(from_prev, from_next, after)


def middle_kernel(e, m, r, *rest):
    nx, ny, nz = e.shape
    arrays = dict(zip(("e", "m", "r") + MADE, (e, m, r) + rest))
    rings = dict(zip(TURNED1, rest[len(MADE) :]))
    slab = Slab(
        lambda name, i, j: (arrays[name], number(i), ROWS * j), lambda name, i: (rings[name], i.slot), ny, nz, None
    )
    strips = range(slab.strips)
    for k in range(RING // 2):
        run(slab.load(Plane(1 + k, k), strips, TURNED1))

    @pl.loop(0, (nx - 2) // RING)
    def _(t):
        for k in range(RING):
            i = Plane(1 + RING * t + k, k)
            run(slab.first(i, strips[1:-1]), slab.load(i.load(RING // 2, nx - 2), strips, TURNED1))


def middle(own):
    nx, ny, nz = own[0].shape
    return pl.pallas_call(
        middle_kernel,
        out_shape=[jax.ShapeDtypeStruct((nx, ny, nz), F32)] * len(MADE),
        in_specs=[VMEM] * 3,
        out_specs=[VMEM] * len(MADE),
        scratch_shapes=[pltpu.VMEM(turned_shape(RING, ny, nz), F32)] * 2,
        compiler_params=pltpu.CompilerParams(vmem_limit_bytes=4 * 2**20),
        cost_estimate=pl.CostEstimate(flops=40 * nx * ny * nz, bytes_accessed=16 * nx * ny * nz, transcendentals=0),
        name="middle",
    )(*own)


def made_place(middles, ends, n, name, i, end, j):
    if 0 < j < n - 1:
        return middles[name], i, ROWS * j
    return ends[name], end, ROWS * {0: 0, n - 1: 1, n: 2}[j]


def inner_kernel(e, m, r, eh, mh, rh, *rest):
    nx, ny, nz = e.shape
    n = ny // ROWS
    own = {"e": (e, eh), "m": (m, mh), "r": (r, rh)}
    count = len(MADE)
    middles, rest = dict(zip(MADE, rest)), rest[count:]
    out_hbm, late, handed, rest = rest[0], rest[1], dict(zip(MADE, rest[2:])), rest[2 + count :]
    ends, rest = dict(zip(MADE, rest)), rest[count:]
    rings, (out, sem) = dict(zip(TURNED1 + TURNED2, rest)), rest[4:]

    def place(name, i, j):
        if name in own:
            ref, strip = own[name]
            return (strip, number(i), 0) if j == n else (ref, number(i), ROWS * j)
        return made_place(middles, ends, n, name, number(i), i.slot, j)

    slab = Slab(place, lambda name, i: (rings[name], i.slot), ny, nz, row_mask())
    around = [0, 1, n - 2, n - 1, n]
    ahead, behind = RING // 2, 3

    def out_copy(i):
        return pltpu.make_async_copy(out.at[i], out_hbm.at[i], sem)

    def second(i):
        return slab.second(i, out, number(i))

    def first(i):
        return [
            slab.first(i, [0, n - 1, n]),
            slab.load(i.load(ahead, nx - 2), around, TURNED1),
            slab.load(i - 1, range(n + 1), TURNED2),
        ]

    def hand(k, slot):
        for name in MADE:
            handed[name][k] = ends[name][slot]

    for k in range(ahead):
        run(slab.load(Plane(1 + k, k), around, TURNED1))
    for k in range(RING):
        i = Plane(1 + k, k)
        if i.number < 2 + behind:
            run(*first(i)[: 2 if k == 0 else 3])
        else:
            run(second(i - behind), *first(i))
            out_copy(i.number - behind).start()
    hand(0, 0)
    hand(1, 1)

    @pl.loop(1, (nx - 2) // RING)
    def _(t):
        for k in range(RING):
            i = Plane(1 + RING * t + k, k)
            run(second(i - behind), *first(i))
            out_copy(i.number - behind).start()

    hand(2, (nx - 4) % RING)
    hand(3, (nx - 3) % RING)
    for k, i in enumerate((nx - 4, nx - 3)):
        run(slab.second(Plane(i, (i - 1) % RING), late, k))
    sent = pl.ds(2, nx - 6)
    pltpu.make_async_copy(out.at[sent], out_hbm.at[sent], sem).wait()


def inner(own, strips, middles):
    nx, ny, nz = own[0].shape
    args = (*own, *strips, *middles)
    return pl.pallas_call(
        inner_kernel,
        out_shape=[jax.ShapeDtypeStruct((nx, ny, nz), F32), jax.ShapeDtypeStruct((2, ny, nz), F32)]
        + [jax.ShapeDtypeStruct((4, 3 * ROWS, nz), F32)] * len(MADE),
        in_specs=[VMEM] * len(args),
        out_specs=[HBM] + [VMEM] * (1 + len(MADE)),
        scratch_shapes=[pltpu.VMEM((RING, 3 * ROWS, nz), F32)] * len(MADE)
        + [pltpu.VMEM(turned_shape(RING, ny, nz), F32)] * 4
        + [pltpu.VMEM((nx, ny, nz), F32), pltpu.SemaphoreType.DMA],
        compiler_params=pltpu.CompilerParams(vmem_limit_bytes=11 * 2**20),
        cost_estimate=pl.CostEstimate(flops=40 * nx * ny * nz, bytes_accessed=16 * nx * ny * nz, transcendentals=0),
        name="inner",
    )(*args)


def outer_kernel(e, m, r, eh, mh, rh, got_out, got_back, corner_out, corner_back, late, *rest):
    nx, ny, nz = e.shape
    n = ny // ROWS
    count = len(MADE)
    middles, ends, rest = dict(zip(MADE, rest)), dict(zip(MADE, rest[count:])), rest[2 * count + 1 :]
    out_hbm, made, rest = rest[0], dict(zip(MADE, rest[1:])), rest[1 + count :]
    rings, (out, sems) = dict(zip(TURNED1 + TURNED2, rest)), rest[4:]
    own = {"e": e, "m": m, "r": r}
    strips = {"e": eh, "m": mh, "r": rh}
    got_at = {("e", -1): 0, ("m", -1): 1, ("m", -2): 2, ("r", -1): 3}
    corner_at = {"e": 0, "m": 1}
    mask = row_mask()
    writes = [pltpu.make_async_copy(late, out_hbm.at[nx - 4 : nx - 2], sems.at[4])]
    writes[0].start()
    for side, (got, corner) in enumerate(((got_out, corner_out), (got_back, corner_back))):
        low = sends_up(side == 1)
        there = jnp.where(low, has_prev("space"), has_next("space"))

        def at(q, low=low):
            return jnp.where(low, q, nx - 1 - q)

        def place(name, q, j, got=got, corner=corner, low=low, at=at):
            if name in own:
                if q >= 0:
                    return (strips[name], at(q), 0) if j == n else (own[name], at(q), ROWS * j)
                if j == n:
                    return corner, corner_at[name], 0
                return got, got_at[name, q], ROWS * j
            if q <= 0:
                return made[name], 1 + q, ROWS * j
            i = jnp.where(low, q, nx - 2 - q) if name == "cx" else at(q)
            end = jnp.where(low, q - 1, 3 - q if name == "cx" else 4 - q)
            return made_place(middles, ends, n, name, i, end, j)

        slab = Slab(place, lambda name, q: (rings[name], q % 2), ny, nz, mask)
        keep = jnp.broadcast_to(jnp.where(there, 1, 0), (ROWS, LANES)) == 1
        run(slab.load(-1, range(n + 1), TURNED1), slab.load(0, range(n + 1), TURNED1))
        run(slab.load(1, range(n + 1), TURNED2))
        run(slab.first(-1, range(n), keep=keep, e_before=False))
        run(slab.first(0, range(n + 1)))
        run(slab.load(0, range(n + 1), TURNED2))
        for q in (0, 1):
            run(slab.second(q, out, 2 * side + q))
            c = pltpu.make_async_copy(out.at[2 * side + q], out_hbm.at[at(q)], sems.at[2 * side + q])
            c.start()
            writes.append(c)
    for c in writes:
        c.wait()


def outer(own, strips, got, corners, late, middles, ends, out):
    nx, ny, nz = own[0].shape
    args = (*own, *strips, *got, *corners, late, *middles, *ends)
    return pl.pallas_call(
        outer_kernel,
        out_shape=jax.ShapeDtypeStruct((nx, ny, nz), F32),
        in_specs=[VMEM] * len(args) + [HBM],
        out_specs=HBM,
        input_output_aliases={len(args): 0},
        scratch_shapes=[pltpu.VMEM((2, ny + ROWS, nz), F32)] * len(MADE)
        + [pltpu.VMEM(turned_shape(2, ny, nz), F32)] * 4
        + [pltpu.VMEM((4, ny, nz), F32), pltpu.SemaphoreType.DMA((5,))],
        compiler_params=pltpu.CompilerParams(vmem_limit_bytes=6 * 2**20),
        name="outer",
    )(*args, out)


def shards(residual, mobility, initial_guess):
    own = (initial_guess, mobility, residual)
    *rows, plane_out, plane_back = send(*(pltpu.with_memory_space_constraint(v, pltpu.HBM) for v in own))
    got = [along_space(v, back) for v, back in ((plane_out, False), (plane_back, True))]
    rows = [along_member(v, back) for v, back in zip(rows, (False, True))]
    middles = middle(own)
    *strips, corner_out, corner_back = halo(*rows, residual.shape[0], middles[-1])
    corners = [along_space(v, back) for v, back in ((corner_out, False), (corner_back, True))]
    out, late, *ends = inner(own, strips, middles)
    return outer(own, strips, got, corners, late, middles, ends, out)


def solution(mesh):
    placed = P("space", "member", None)
    return jax.shard_map(shards, mesh=mesh, in_specs=(placed,) * 3, out_specs=placed, check_vma=False)
```

```python
import math

import jax
import jax.numpy as jnp
from jax import lax
from jax.experimental import pallas as pl
from jax.experimental.pallas import tpu as pltpu
from jax.sharding import PartitionSpec as P

sweep_weights = tuple((1.0 / (1.15 + 0.85 * math.cos(math.pi * (2 * j - 1) / 4.0)) for j in (1, 2)))

LANES = 128
ROWS = 8
VMEM = pl.BlockSpec(memory_space=pltpu.VMEM)
HBM = pl.BlockSpec(memory_space=pltpu.HBM)
F32 = jnp.float32


def lane_slices(nz):
    return [slice(k * LANES, (k + 1) * LANES) for k in range(nz // LANES)]


def iotas():
    row = lax.broadcasted_iota(jnp.int32, (ROWS, LANES), 0)
    lane = lax.broadcasted_iota(jnp.int32, (ROWS, LANES), 1)
    return row, lane


def next_lanes(vals, last_lane):
    turned = [pltpu.roll(v, LANES - 1, 1) for v in vals]
    return [jnp.where(last_lane, b, a) for a, b in zip(turned, turned[1:] + [0.0])]


def prev_lanes(vals, first_lane):
    turned = [pltpu.roll(v, 1, 1) for v in vals]
    return [jnp.where(first_lane, b, a) for a, b in zip(turned, [0.0] + turned[:-1])]


class Slab:
    def __init__(self, place, turning, ny, nz, row_ok):
        self.place, self.turning = place, turning
        self.strips = ny // ROWS
        self.tiles = lane_slices(nz)
        self.row_ok = row_ok
        _, lane = iotas()
        self.first_lane, self.last_lane = lane == 0, lane == LANES - 1

    def get(self, name, i, j):
        ref, at, row = self.place(name, i, j)
        return [ref[at, row : row + ROWS, s] for s in self.tiles]

    def put(self, name, i, j, vals):
        ref, at, row = self.place(name, i, j)
        for s, v in zip(self.tiles, vals):
            ref[at, row : row + ROWS, s] = v

    def load(self, i, strips, names):
        for j in strips:
            for name in names:
                ref, at = self.turning(name, i)
                vals = self.get(name, i, j)
                for row in (0, ROWS * (j + 1)) if j == self.strips else (ROWS * (j + 1),):
                    for k, v in enumerate(vals):
                        ref[at, k, row : row + ROWS, :] = v
            yield

    def shifted(self, name, i, j, by=0):
        ref, at = self.turning(name, i)
        if j == self.strips:
            row = {0: 0, 1: 1, -1: ROWS * (j + 1) - 1}[by]
        else:
            row = ROWS * (j + 1) + by
        return [ref[at, k, row : row + ROWS, :] for k in range(len(self.tiles))]

    def first(self, i, strips, keep=None, e_before=True):
        w = sweep_weights[0]
        n = self.strips
        strips = list(strips)

        def ahead(j):
            e, m = self.shifted("e", i, j), self.shifted("m", i, j)
            return (
                e,
                m,
                next_lanes(e, self.last_lane),
                prev_lanes(e, self.first_lane),
                next_lanes(m, self.last_lane),
                prev_lanes(m, self.first_lane),
            )

        here = ahead(strips[0])
        for j, after in zip(strips, strips[1:] + [None]):
            there = None if after is None else ahead(after)
            e, m, e_zp, e_zm, m_zp, m_zm = here
            e_up, e_dn = self.shifted("e", i, j, 1), self.shifted("e", i, j, -1)
            m_up, m_dn = self.shifted("m", i, j, 1), self.shifted("m", i, j, -1)
            e_xp, e_xm = self.get("e", i + 1, j), self.get("e", i - 1, j) if e_before else None
            m_xp, m_xm = self.get("m", i + 1, j), self.get("m", i - 1, j)
            r = self.get("r", i, j)
            made = []
            for k in range(len(self.tiles)):
                cx, cxm = m[k] + m_xp[k], m[k] + m_xm[k]
                cy, cy_dn = m[k] + m_up[k], m[k] + m_dn[k]
                cz, cz_dn = m[k] + m_zp[k], m[k] + m_zm[k]
                t = ((cx + cxm) + (cy + cy_dn)) + (cz + cz_dn)
                num_x = cx * e_xp[k] + cxm * e_xm[k] if e_before else cx * e_xp[k]
                num = (num_x + (cy * e_up[k] + cy_dn * e_dn[k])) + ((cz * e_zp[k] + cz_dn * e_zm[k]) + (r[k] + r[k]))
                rt = 1.0 / t
                e1 = (1.0 - w) * e[k] + (w * rt) * num
                if j == n:
                    e1 = jnp.where(self.row_ok, e1, 0.0)
                if keep is not None:
                    e1 = jnp.where(keep, e1, 0.0)
                made.append((cx, cy, cz, rt, e1))
            cx, cy, cz, rt, e1 = zip(*made)
            self.put("cy", i, j, cy)
            self.put("e1", i, j, e1)
            if j < n:
                self.put("cx", i, j, cx)
                self.put("cz", i, j, cz)
                self.put("rt", i, j, rt)
            here = there
            yield

    def second(self, i, out, o):
        w = sweep_weights[1]

        def ahead(j):
            e, cz = self.shifted("e1", i, j), self.get("cz", i, j)
            return e, cz, next_lanes(e, self.last_lane), prev_lanes([a * b for a, b in zip(cz, e)], self.first_lane)

        here = ahead(0)
        for j in range(self.strips):
            there = ahead(j + 1) if j < self.strips - 1 else None
            e, cz, e_zp, h_dn = here
            e_up, e_dn = self.shifted("e1", i, j, 1), self.shifted("e1", i, j, -1)
            cy, cy_dn = self.shifted("cy", i, j), self.shifted("cy", i, j, -1)
            e_xp, e_xm = self.get("e1", i + 1, j), self.get("e1", i - 1, j)
            cx, cxm = self.get("cx", i, j), self.get("cx", i - 1, j)
            rt = self.get("rt", i, j)
            r = self.get("r", i, j)
            outs = []
            for k in range(len(self.tiles)):
                num = ((cx[k] * e_xp[k] + cxm[k] * e_xm[k]) + (cy[k] * e_up[k] + cy_dn[k] * e_dn[k])) + (
                    (cz[k] * e_zp[k] + h_dn[k]) + (r[k] + r[k])
                )
                outs.append((1.0 - w) * e[k] + (w * rt[k]) * num)
            for s, v in zip(self.tiles, outs):
                out[o, ROWS * j : ROWS * (j + 1), s] = v
            here = there
            yield


def run(*passes):
    passes = list(passes)
    while passes:
        passes = [p for p in passes if next(p, StopIteration) is not StopIteration]


RING = 6
MIDDLE_RING = 10
TURNED1, TURNED2 = ("e", "m"), ("e1", "cy")
MADE = ("e1", "cy", "cx", "cz", "rt")


def turned_shape(planes, ny, nz):
    return (planes, nz // LANES, ny + 2 * ROWS, LANES)


class Plane:
    def __init__(self, number, slot, ring=RING):
        self.number, self.slot, self.ring = number, slot % ring, ring

    def __add__(self, by):
        return Plane(self.number + by, self.slot + by, self.ring)

    def __sub__(self, by):
        return self + -by

    def load(self, by, last):
        return Plane(jnp.minimum(self.number + by, last), self.slot + by, self.ring)


def number(i):
    return i.number if isinstance(i, Plane) else i


def along_space(x, back):
    ns, nm = lax.axis_size("space"), lax.axis_size("member")
    hops = []
    for m in range(nm):
        step = 1 if m % 2 == 0 else -1
        for i in range(ns):
            to = (i + step, m) if 0 <= i + step < ns else (i, m + step)
            hops.append((i * nm + m, to[0] * nm + to[1]))
    return lax.ppermute(x, ("space", "member"), [(b, a) for a, b in hops] if back else hops)


def along_member(x, back):
    n = lax.axis_size("member")
    return lax.ppermute(x, "member", [((i + 1) % n, i) if back else (i, (i + 1) % n) for i in range(n)])


def sends_up(back):
    even = lax.rem(lax.axis_index("member"), 2) == 0
    return jnp.logical_not(even) if back else even


def has_next(axis):
    return lax.axis_index(axis) < lax.axis_size(axis) - 1


def has_prev(axis):
    return lax.axis_index(axis) > 0


def row_mask():
    row, _ = iotas()
    after, before = jnp.where(has_next("member"), 1, 0), jnp.where(has_prev("member"), 1, 0)
    return jnp.where(row < ROWS // 2, after, before) == 1


def with_behind(e_behind, m_behind, m, r):
    return r + (0.5 * e_behind) * (m + m_behind)


def send_kernel(e, m, r, to_next, to_prev, plane_out, plane_back, top, bottom, planes, sems, plane_sems):
    nx, ny, nz = e.shape
    groups = nx // ROWS
    reads = []
    for k, src in enumerate((e, m, r)):
        for dst, at in ((top, 0), (bottom, ny - ROWS)):
            rows = 1 if k == 2 else 2
            first = 0 if at == 0 else ROWS - rows
            here, there = src.at[:, at + first : at + first + rows], dst.at[k, :, first : first + rows]
            reads.append(pltpu.make_async_copy(here, there, sems.at[len(reads)]))
    for c in reads:
        c.start()
    reads2 = []
    for side, (dst, back) in enumerate(((plane_out, False), (plane_back, True))):
        up = sends_up(back)
        end, behind = jnp.where(up, nx - 1, 0), jnp.where(up, nx - 2, 1)
        for src, at, to in (
            (e, end, dst.at[0]),
            (m, end, dst.at[1]),
            (m, behind, dst.at[2]),
            (e, behind, planes.at[2 * side]),
            (r, end, planes.at[2 * side + 1]),
        ):
            reads2.append(pltpu.make_async_copy(src.at[at], to, plane_sems.at[len(reads2)]))
    for c in reads2:
        c.start()
    for c in reads:
        c.wait()
    next_ok, prev_ok = has_next("member"), has_prev("member")
    for dst, strips, end, behind, ok in (
        (to_next, bottom, ROWS - 1, ROWS - 2, next_ok),
        (to_prev, top, 0, 1, prev_ok),
    ):
        for g in range(groups):
            at = slice(ROWS * g, ROWS * (g + 1))
            e_behind, m_behind = strips[0, at, behind, :], strips[1, at, behind, :]
            e_end, m_end, r_end = (strips[k, at, end, :] for k in range(3))
            for n, v in enumerate((e_end, m_end, m_behind, with_behind(e_behind, m_behind, m_end, r_end))):
                dst[groups * n + g] = jnp.where(ok, v, 0.0)
    for c in reads2:
        c.wait()
    for side, (dst, back) in enumerate(((plane_out, False), (plane_back, True))):

        @pl.loop(0, ny // ROWS)
        def _(j, side=side, dst=dst):
            at = pl.ds(pl.multiple_of(j * ROWS, ROWS), ROWS)
            dst[3, at, :] = with_behind(planes[2 * side, at, :], dst[2, at, :], dst[1, at, :], planes[2 * side + 1, at, :])

        @pl.when(jnp.logical_not(jnp.where(sends_up(back), has_next("space"), has_prev("space"))))
        def _(dst=dst):
            dst[...] = jnp.zeros_like(dst)


def send(e, m, r):
    nx, ny, nz = e.shape
    rows = jax.ShapeDtypeStruct((4 * (nx // ROWS), ROWS, nz), F32)
    planes = jax.ShapeDtypeStruct((4, ny, nz), F32)
    strips = pltpu.VMEM((3, nx, ROWS, nz), F32)
    return pl.pallas_call(
        send_kernel,
        out_shape=[rows, rows, planes, planes],
        in_specs=[HBM] * 3,
        out_specs=[VMEM] * 4,
        scratch_shapes=[strips, strips, pltpu.VMEM((4, ny, nz), F32)]
        + [pltpu.SemaphoreType.DMA((6,)), pltpu.SemaphoreType.DMA((10,))],
        compiler_params=pltpu.CompilerParams(vmem_limit_bytes=8 * 2**20),
        name="send",
    )(e, m, r)


def halo_kernel(from_prev, from_next, _, eh, mh, rh, corner_out, corner_back):
    nx, _, nz = eh.shape
    groups = nx // ROWS
    for ref in (eh, mh, rh):
        ref[...] = jnp.zeros_like(ref)
    for n, (ref, below, above) in enumerate(((eh, 1, 0), (mh, 1, 0), (mh, 2, 1), (rh, 1, 0))):
        for g in range(groups):
            at = slice(ROWS * g, ROWS * (g + 1))
            ref[at, ROWS - below, :] = from_prev[groups * n + g]
            ref[at, above, :] = from_next[groups * n + g]
    for dst, back in ((corner_out, False), (corner_back, True)):
        up = sends_up(back)
        ok = jnp.where(up, has_next("space"), has_prev("space"))
        at = jnp.where(up, nx - 1, 0)
        dst[0] = jnp.where(ok, eh[at], 0.0)
        dst[1] = jnp.where(ok, mh[at], 0.0)


def halo(from_prev, from_next, nx, after):
    nz = from_prev.shape[2]
    strip = jax.ShapeDtypeStruct((nx, ROWS, nz), F32)
    corner = jax.ShapeDtypeStruct((2, ROWS, nz), F32)
    return pl.pallas_call(
        halo_kernel,
        out_shape=[strip] * 3 + [corner] * 2,
        in_specs=[VMEM] * 2 + [pl.BlockSpec(memory_space=pl.ANY)],
        out_specs=[VMEM] * 5,
        compiler_params=pltpu.CompilerParams(vmem_limit_bytes=2 * 2**20),
        name="halo",
    )(from_prev, from_next, after)


def middle_kernel(e, m, r, *rest):
    nx, ny, nz = e.shape
    arrays = dict(zip(("e", "m", "r") + MADE, (e, m, r) + rest))
    rings = dict(zip(TURNED1, rest[len(MADE) :]))
    slab = Slab(
        lambda name, i, j: (arrays[name], number(i), ROWS * j), lambda name, i: (rings[name], i.slot), ny, nz, None
    )
    strips = range(slab.strips)
    for k in range(3):
        run(slab.load(Plane(1 + k, k, MIDDLE_RING), strips, TURNED1))

    @pl.loop(0, (nx - 2) // MIDDLE_RING)
    def _(t):
        for k in range(MIDDLE_RING):
            i = Plane(1 + MIDDLE_RING * t + k, k, MIDDLE_RING)
            run(slab.first(i, strips[1:-1]), slab.load(i.load(3, nx - 2), strips, TURNED1))


def middle(own):
    nx, ny, nz = own[0].shape
    return pl.pallas_call(
        middle_kernel,
        out_shape=[jax.ShapeDtypeStruct((nx, ny, nz), F32)] * len(MADE),
        in_specs=[VMEM] * 3,
        out_specs=[VMEM] * len(MADE),
        scratch_shapes=[pltpu.VMEM(turned_shape(MIDDLE_RING, ny, nz), F32)] * 2,
        compiler_params=pltpu.CompilerParams(vmem_limit_bytes=5 * 2**20),
        cost_estimate=pl.CostEstimate(flops=40 * nx * ny * nz, bytes_accessed=16 * nx * ny * nz, transcendentals=0),
        name="middle",
    )(*own)


def made_place(middles, ends, n, name, i, end, j):
    if 0 < j < n - 1:
        return middles[name], i, ROWS * j
    return ends[name], end, ROWS * {0: 0, n - 1: 1, n: 2}[j]


def inner_kernel(e, m, r, eh, mh, rh, *rest):
    nx, ny, nz = e.shape
    n = ny // ROWS
    own = {"e": (e, eh), "m": (m, mh), "r": (r, rh)}
    count = len(MADE)
    middles, rest = dict(zip(MADE, rest)), rest[count:]
    out_hbm, out, handed, rest = rest[0], rest[1], dict(zip(MADE, rest[2:])), rest[2 + count :]
    ends, rest = dict(zip(MADE, rest)), rest[count:]
    rings, (sem,) = dict(zip(TURNED1 + TURNED2, rest)), rest[4:]

    def place(name, i, j):
        if name in own:
            ref, strip = own[name]
            return (strip, number(i), 0) if j == n else (ref, number(i), ROWS * j)
        return made_place(middles, ends, n, name, number(i), i.slot, j)

    slab = Slab(place, lambda name, i: (rings[name], i.slot), ny, nz, row_mask())
    around = [0, 1, n - 2, n - 1, n]
    ahead, behind = RING // 2, 3

    def send_out(first, count):
        at = pl.ds(first, count)
        return pltpu.make_async_copy(out.at[at], out_hbm.at[at], sem)

    def second(i):
        return slab.second(i, out, number(i))

    def first(i):
        return [
            slab.first(i, [0, n - 1, n]),
            slab.load(i.load(ahead, nx - 2), around, TURNED1),
            slab.load(i - 1, range(n + 1), TURNED2),
        ]

    def hand(k, slot):
        for name in MADE:
            handed[name][k] = ends[name][slot]

    for k in range(ahead):
        run(slab.load(Plane(1 + k, k), around, TURNED1))
    for k in range(RING):
        i = Plane(1 + k, k)
        if i.number < 2 + behind:
            run(*first(i)[: 2 if k == 0 else 3])
        else:
            run(second(i - behind), *first(i))
    hand(0, 0)
    hand(1, 1)
    send_out(2, 2).start()

    @pl.loop(1, (nx - 2) // RING)
    def _(t):
        @pl.when(t > 1)
        def _():
            send_out(4 + RING * (t - 2), RING).start()

        for k in range(RING):
            i = Plane(1 + RING * t + k, k)
            run(second(i - behind), *first(i))

    hand(2, (nx - 4) % RING)
    hand(3, (nx - 3) % RING)
    for i in (nx - 4, nx - 3):
        run(second(Plane(i, i - 1)))
    send_out(2, unsent(nx) - 2).wait()


def unsent(nx):
    return max(4, nx - 4 - RING)


def inner(own, strips, middles):
    nx, ny, nz = own[0].shape
    args = (*own, *strips, *middles)
    return pl.pallas_call(
        inner_kernel,
        out_shape=[jax.ShapeDtypeStruct((nx, ny, nz), F32)] * 2
        + [jax.ShapeDtypeStruct((4, 3 * ROWS, nz), F32)] * len(MADE),
        in_specs=[VMEM] * len(args),
        out_specs=[HBM] + [VMEM] * (1 + len(MADE)),
        scratch_shapes=[pltpu.VMEM((RING, 3 * ROWS, nz), F32)] * len(MADE)
        + [pltpu.VMEM(turned_shape(RING, ny, nz), F32)] * 4
        + [pltpu.SemaphoreType.DMA],
        compiler_params=pltpu.CompilerParams(vmem_limit_bytes=7 * 2**20),
        cost_estimate=pl.CostEstimate(flops=40 * nx * ny * nz, bytes_accessed=16 * nx * ny * nz, transcendentals=0),
        name="inner",
    )(*args)


def outer_kernel(e, m, r, eh, mh, rh, got_out, got_back, corner_out, corner_back, second, *rest):
    nx, ny, nz = e.shape
    n = ny // ROWS
    count = len(MADE)
    middles, ends, rest = dict(zip(MADE, rest)), dict(zip(MADE, rest[count:])), rest[2 * count + 1 :]
    out_hbm, made, rest = rest[0], dict(zip(MADE, rest[1:])), rest[1 + count :]
    rings, (out, sems) = dict(zip(TURNED1 + TURNED2, rest)), rest[4:]
    own = {"e": e, "m": m, "r": r}
    strips = {"e": eh, "m": mh, "r": rh}
    got_at = {("e", -1): 0, ("m", -1): 1, ("m", -2): 2, ("r", -1): 3}
    corner_at = {"e": 0, "m": 1}
    mask = row_mask()
    late = pl.ds(unsent(nx), nx - 2 - unsent(nx))
    writes = [pltpu.make_async_copy(second.at[late], out_hbm.at[late], sems.at[4])]
    writes[0].start()
    for side, (got, corner) in enumerate(((got_out, corner_out), (got_back, corner_back))):
        low = sends_up(side == 1)
        there = jnp.where(low, has_prev("space"), has_next("space"))

        def at(q, low=low):
            return jnp.where(low, q, nx - 1 - q)

        def place(name, q, j, got=got, corner=corner, low=low, at=at):
            if name in own:
                if q >= 0:
                    return (strips[name], at(q), 0) if j == n else (own[name], at(q), ROWS * j)
                if j == n:
                    return corner, corner_at[name], 0
                return got, got_at[name, q], ROWS * j
            if q <= 0:
                return made[name], 1 + q, ROWS * j
            i = jnp.where(low, q, nx - 2 - q) if name == "cx" else at(q)
            end = jnp.where(low, q - 1, 3 - q if name == "cx" else 4 - q)
            return made_place(middles, ends, n, name, i, end, j)

        slab = Slab(place, lambda name, q: (rings[name], q % 2), ny, nz, mask)
        keep = jnp.broadcast_to(jnp.where(there, 1, 0), (ROWS, LANES)) == 1
        run(slab.load(-1, range(n + 1), TURNED1), slab.load(0, range(n + 1), TURNED1))
        run(slab.load(1, range(n + 1), TURNED2))
        run(slab.first(-1, range(n), keep=keep, e_before=False))
        run(slab.first(0, range(n + 1)))
        run(slab.load(0, range(n + 1), TURNED2))
        for q in (0, 1):
            run(slab.second(q, out, 2 * side + q))
            c = pltpu.make_async_copy(out.at[2 * side + q], out_hbm.at[at(q)], sems.at[2 * side + q])
            c.start()
            writes.append(c)
    for c in writes:
        c.wait()


def outer(own, strips, got, corners, second, middles, ends, out):
    nx, ny, nz = own[0].shape
    args = (*own, *strips, *got, *corners, second, *middles, *ends)
    return pl.pallas_call(
        outer_kernel,
        out_shape=jax.ShapeDtypeStruct((nx, ny, nz), F32),
        in_specs=[VMEM] * len(args) + [HBM],
        out_specs=HBM,
        input_output_aliases={len(args): 0},
        scratch_shapes=[pltpu.VMEM((2, ny + ROWS, nz), F32)] * len(MADE)
        + [pltpu.VMEM(turned_shape(2, ny, nz), F32)] * 4
        + [pltpu.VMEM((4, ny, nz), F32), pltpu.SemaphoreType.DMA((5,))],
        compiler_params=pltpu.CompilerParams(vmem_limit_bytes=6 * 2**20),
        name="outer",
    )(*args, out)


def shards(residual, mobility, initial_guess):
    own = (initial_guess, mobility, residual)
    *rows, plane_out, plane_back = send(*(pltpu.with_memory_space_constraint(v, pltpu.HBM) for v in own))
    got = [along_space(v, back) for v, back in ((plane_out, False), (plane_back, True))]
    rows = [along_member(v, back) for v, back in zip(rows, (False, True))]
    middles = middle(own)
    *strips, corner_out, corner_back = halo(*rows, residual.shape[0], middles[-1])
    corners = [along_space(v, back) for v, back in ((corner_out, False), (corner_back, True))]
    out, second, *ends = inner(own, strips, middles)
    return outer(own, strips, got, corners, second, middles, ends, out)


def solution(mesh):
    placed = P("space", "member", None)
    return jax.shard_map(shards, mesh=mesh, in_specs=(placed,) * 3, out_specs=placed, check_vma=False)
```

```python
import math

import jax
import jax.numpy as jnp
from jax import lax
from jax.experimental import pallas as pl
from jax.experimental.pallas import tpu as pltpu
from jax.sharding import PartitionSpec as P

sweep_weights = tuple((1.0 / (1.15 + 0.85 * math.cos(math.pi * (2 * j - 1) / 4.0)) for j in (1, 2)))

LANES = 128
ROWS = 8
VMEM = pl.BlockSpec(memory_space=pltpu.VMEM)
HBM = pl.BlockSpec(memory_space=pltpu.HBM)
F32 = jnp.float32


def lane_slices(nz):
    return [slice(k * LANES, (k + 1) * LANES) for k in range(nz // LANES)]


def iotas():
    row = lax.broadcasted_iota(jnp.int32, (ROWS, LANES), 0)
    lane = lax.broadcasted_iota(jnp.int32, (ROWS, LANES), 1)
    return row, lane


def next_lanes(vals, last_lane):
    turned = [pltpu.roll(v, LANES - 1, 1) for v in vals]
    return [jnp.where(last_lane, b, a) for a, b in zip(turned, turned[1:] + [0.0])]


def prev_lanes(vals, first_lane):
    turned = [pltpu.roll(v, 1, 1) for v in vals]
    return [jnp.where(first_lane, b, a) for a, b in zip(turned, [0.0] + turned[:-1])]


class Slab:
    def __init__(self, place, turning, ny, nz, row_ok):
        self.place, self.turning = place, turning
        self.strips = ny // ROWS
        self.tiles = lane_slices(nz)
        self.row_ok = row_ok
        _, lane = iotas()
        self.first_lane, self.last_lane = lane == 0, lane == LANES - 1

    def get(self, name, i, j):
        ref, at, row = self.place(name, i, j)
        return [ref[at, row : row + ROWS, s] for s in self.tiles]

    def put(self, name, i, j, vals):
        ref, at, row = self.place(name, i, j)
        for s, v in zip(self.tiles, vals):
            ref[at, row : row + ROWS, s] = v

    def load(self, i, strips, names):
        for j in strips:
            for name in names:
                ref, at = self.turning(name, i)
                vals = self.get(name, i, j)
                for row in (0, ROWS * (j + 1)) if j == self.strips else (ROWS * (j + 1),):
                    for k, v in enumerate(vals):
                        ref[at, k, row : row + ROWS, :] = v
            yield

    def shifted(self, name, i, j, by=0):
        ref, at = self.turning(name, i)
        if j == self.strips:
            row = {0: 0, 1: 1, -1: ROWS * (j + 1) - 1}[by]
        else:
            row = ROWS * (j + 1) + by
        return [ref[at, k, row : row + ROWS, :] for k in range(len(self.tiles))]

    def first(self, i, strips, keep=None, e_before=True):
        w = sweep_weights[0]
        n = self.strips
        strips = list(strips)

        def ahead(j):
            e, m = self.shifted("e", i, j), self.shifted("m", i, j)
            return (
                e,
                m,
                next_lanes(e, self.last_lane),
                prev_lanes(e, self.first_lane),
                next_lanes(m, self.last_lane),
                prev_lanes(m, self.first_lane),
            )

        here = ahead(strips[0])
        for j, after in zip(strips, strips[1:] + [None]):
            there = None if after is None else ahead(after)
            e, m, e_zp, e_zm, m_zp, m_zm = here
            e_up, e_dn = self.shifted("e", i, j, 1), self.shifted("e", i, j, -1)
            m_up, m_dn = self.shifted("m", i, j, 1), self.shifted("m", i, j, -1)
            e_xp, e_xm = self.get("e", i + 1, j), self.get("e", i - 1, j) if e_before else None
            m_xp, m_xm = self.get("m", i + 1, j), self.get("m", i - 1, j)
            r = self.get("r", i, j)
            made = []
            for k in range(len(self.tiles)):
                cx, cxm = m[k] + m_xp[k], m[k] + m_xm[k]
                cy, cy_dn = m[k] + m_up[k], m[k] + m_dn[k]
                cz, cz_dn = m[k] + m_zp[k], m[k] + m_zm[k]
                t = ((cx + cxm) + (cy + cy_dn)) + (cz + cz_dn)
                num_x = cx * e_xp[k] + cxm * e_xm[k] if e_before else cx * e_xp[k]
                num = (num_x + (cy * e_up[k] + cy_dn * e_dn[k])) + ((cz * e_zp[k] + cz_dn * e_zm[k]) + (r[k] + r[k]))
                rt = 1.0 / t
                e1 = (1.0 - w) * e[k] + (w * rt) * num
                if j == n:
                    e1 = jnp.where(self.row_ok, e1, 0.0)
                if keep is not None:
                    e1 = jnp.where(keep, e1, 0.0)
                made.append((cx, cy, cz, rt, e1))
            cx, cy, cz, rt, e1 = zip(*made)
            self.put("cy", i, j, cy)
            self.put("e1", i, j, e1)
            if j < n:
                self.put("cx", i, j, cx)
                self.put("cz", i, j, cz)
                self.put("rt", i, j, rt)
            here = there
            yield

    def second(self, i, out, o):
        w = sweep_weights[1]

        def ahead(j):
            e, cz = self.shifted("e1", i, j), self.get("cz", i, j)
            return e, cz, next_lanes(e, self.last_lane), prev_lanes([a * b for a, b in zip(cz, e)], self.first_lane)

        here = ahead(0)
        for j in range(self.strips):
            there = ahead(j + 1) if j < self.strips - 1 else None
            e, cz, e_zp, h_dn = here
            e_up, e_dn = self.shifted("e1", i, j, 1), self.shifted("e1", i, j, -1)
            cy, cy_dn = self.shifted("cy", i, j), self.shifted("cy", i, j, -1)
            e_xp, e_xm = self.get("e1", i + 1, j), self.get("e1", i - 1, j)
            cx, cxm = self.get("cx", i, j), self.get("cx", i - 1, j)
            rt = self.get("rt", i, j)
            r = self.get("r", i, j)
            outs = []
            for k in range(len(self.tiles)):
                num = ((cx[k] * e_xp[k] + cxm[k] * e_xm[k]) + (cy[k] * e_up[k] + cy_dn[k] * e_dn[k])) + (
                    (cz[k] * e_zp[k] + h_dn[k]) + (r[k] + r[k])
                )
                outs.append((1.0 - w) * e[k] + (w * rt[k]) * num)
            for s, v in zip(self.tiles, outs):
                out[o, ROWS * j : ROWS * (j + 1), s] = v
            here = there
            yield


def run(*passes):
    passes = list(passes)
    while passes:
        passes = [p for p in passes if next(p, StopIteration) is not StopIteration]


RING = 6
MIDDLE_RING = 10
TURNED1, TURNED2 = ("e", "m"), ("e1", "cy")
MADE = ("e1", "cy", "cx", "cz", "rt")


def turned_shape(planes, ny, nz):
    return (planes, nz // LANES, ny + 2 * ROWS, LANES)


class Plane:
    def __init__(self, number, slot, ring=RING):
        self.number, self.slot, self.ring = number, slot % ring, ring

    def __add__(self, by):
        return Plane(self.number + by, self.slot + by, self.ring)

    def __sub__(self, by):
        return self + -by

    def load(self, by, last):
        return Plane(jnp.minimum(self.number + by, last), self.slot + by, self.ring)


def number(i):
    return i.number if isinstance(i, Plane) else i


def along_space(x, back):
    ns, nm = lax.axis_size("space"), lax.axis_size("member")
    hops = []
    for m in range(nm):
        step = 1 if m % 2 == 0 else -1
        for i in range(ns):
            to = (i + step, m) if 0 <= i + step < ns else (i, m + step)
            hops.append((i * nm + m, to[0] * nm + to[1]))
    return lax.ppermute(x, ("space", "member"), [(b, a) for a, b in hops] if back else hops)


def along_member(x, back):
    n = lax.axis_size("member")
    return lax.ppermute(x, "member", [((i + 1) % n, i) if back else (i, (i + 1) % n) for i in range(n)])


def sends_up(back):
    even = lax.rem(lax.axis_index("member"), 2) == 0
    return jnp.logical_not(even) if back else even


def has_next(axis):
    return lax.axis_index(axis) < lax.axis_size(axis) - 1


def has_prev(axis):
    return lax.axis_index(axis) > 0


def row_mask():
    row, _ = iotas()
    after, before = jnp.where(has_next("member"), 1, 0), jnp.where(has_prev("member"), 1, 0)
    return jnp.where(row < ROWS // 2, after, before) == 1


def with_behind(e_behind, m_behind, m, r):
    return r + (0.5 * e_behind) * (m + m_behind)


def send_kernel(e, m, r, to_next, to_prev, plane_out, plane_back, top, bottom, planes, sems, plane_sems):
    nx, ny, nz = e.shape
    groups = nx // ROWS
    reads = []
    for k, src in enumerate((e, m, r)):
        for dst, at in ((top, 0), (bottom, ny - ROWS)):
            rows = 1 if k == 2 else 2
            first = 0 if at == 0 else ROWS - rows
            here, there = src.at[:, at + first : at + first + rows], dst.at[k, :, first : first + rows]
            reads.append(pltpu.make_async_copy(here, there, sems.at[len(reads)]))
    for c in reads:
        c.start()
    reads2 = []
    for side, (dst, back) in enumerate(((plane_out, False), (plane_back, True))):
        up = sends_up(back)
        end, behind = jnp.where(up, nx - 1, 0), jnp.where(up, nx - 2, 1)
        for src, at, to in (
            (e, end, dst.at[0]),
            (m, end, dst.at[1]),
            (m, behind, dst.at[2]),
            (e, behind, planes.at[2 * side]),
            (r, end, planes.at[2 * side + 1]),
        ):
            reads2.append(pltpu.make_async_copy(src.at[at], to, plane_sems.at[len(reads2)]))
    for c in reads2:
        c.start()
    for c in reads:
        c.wait()
    next_ok, prev_ok = has_next("member"), has_prev("member")
    for dst, strips, end, behind, ok in (
        (to_next, bottom, ROWS - 1, ROWS - 2, next_ok),
        (to_prev, top, 0, 1, prev_ok),
    ):
        for g in range(groups):
            at = slice(ROWS * g, ROWS * (g + 1))
            e_behind, m_behind = strips[0, at, behind, :], strips[1, at, behind, :]
            e_end, m_end, r_end = (strips[k, at, end, :] for k in range(3))
            for n, v in enumerate((e_end, m_end, m_behind, with_behind(e_behind, m_behind, m_end, r_end))):
                dst[groups * n + g] = jnp.where(ok, v, 0.0)
    for c in reads2:
        c.wait()
    for side, (dst, back) in enumerate(((plane_out, False), (plane_back, True))):

        @pl.loop(0, ny // ROWS)
        def _(j, side=side, dst=dst):
            at = pl.ds(pl.multiple_of(j * ROWS, ROWS), ROWS)
            dst[3, at, :] = with_behind(planes[2 * side, at, :], dst[2, at, :], dst[1, at, :], planes[2 * side + 1, at, :])

        @pl.when(jnp.logical_not(jnp.where(sends_up(back), has_next("space"), has_prev("space"))))
        def _(dst=dst):
            dst[...] = jnp.zeros_like(dst)


def send(e, m, r):
    nx, ny, nz = e.shape
    rows = jax.ShapeDtypeStruct((4 * (nx // ROWS), ROWS, nz), F32)
    planes = jax.ShapeDtypeStruct((4, ny, nz), F32)
    strips = pltpu.VMEM((3, nx, ROWS, nz), F32)
    return pl.pallas_call(
        send_kernel,
        out_shape=[rows, rows, planes, planes],
        in_specs=[HBM] * 3,
        out_specs=[VMEM] * 4,
        scratch_shapes=[strips, strips, pltpu.VMEM((4, ny, nz), F32)]
        + [pltpu.SemaphoreType.DMA((6,)), pltpu.SemaphoreType.DMA((10,))],
        compiler_params=pltpu.CompilerParams(vmem_limit_bytes=8 * 2**20),
        name="send",
    )(e, m, r)


def halo_kernel(from_prev, from_next, _, eh, mh, rh, corner_out, corner_back):
    nx, _, nz = eh.shape
    groups = nx // ROWS
    for ref in (eh, mh, rh):
        ref[...] = jnp.zeros_like(ref)
    for n, (ref, below, above) in enumerate(((eh, 1, 0), (mh, 1, 0), (mh, 2, 1), (rh, 1, 0))):
        for g in range(groups):
            at = slice(ROWS * g, ROWS * (g + 1))
            ref[at, ROWS - below, :] = from_prev[groups * n + g]
            ref[at, above, :] = from_next[groups * n + g]
    for dst, back in ((corner_out, False), (corner_back, True)):
        up = sends_up(back)
        ok = jnp.where(up, has_next("space"), has_prev("space"))
        at = jnp.where(up, nx - 1, 0)
        dst[0] = jnp.where(ok, eh[at], 0.0)
        dst[1] = jnp.where(ok, mh[at], 0.0)


def halo(from_prev, from_next, nx, after):
    nz = from_prev.shape[2]
    strip = jax.ShapeDtypeStruct((nx, ROWS, nz), F32)
    corner = jax.ShapeDtypeStruct((2, ROWS, nz), F32)
    return pl.pallas_call(
        halo_kernel,
        out_shape=[strip] * 3 + [corner] * 2,
        in_specs=[VMEM] * 2 + [pl.BlockSpec(memory_space=pl.ANY)],
        out_specs=[VMEM] * 5,
        compiler_params=pltpu.CompilerParams(vmem_limit_bytes=2 * 2**20),
        name="halo",
    )(from_prev, from_next, after)


def middle_kernel(e, m, r, *rest):
    nx, ny, nz = e.shape
    arrays = dict(zip(("e", "m", "r") + MADE, (e, m, r) + rest))
    rings = dict(zip(TURNED1, rest[len(MADE) :]))
    slab = Slab(
        lambda name, i, j: (arrays[name], number(i), ROWS * j), lambda name, i: (rings[name], i.slot), ny, nz, None
    )
    strips = range(slab.strips)
    for k in range(3):
        run(slab.load(Plane(1 + k, k, MIDDLE_RING), strips, TURNED1))

    @pl.loop(0, (nx - 2) // MIDDLE_RING)
    def _(t):
        for k in range(MIDDLE_RING):
            i = Plane(1 + MIDDLE_RING * t + k, k, MIDDLE_RING)
            run(slab.first(i, strips[1:-1]), slab.load(i.load(3, nx - 2), strips, TURNED1))


def middle(own):
    nx, ny, nz = own[0].shape
    return pl.pallas_call(
        middle_kernel,
        out_shape=[jax.ShapeDtypeStruct((nx, ny, nz), F32)] * len(MADE),
        in_specs=[VMEM] * 3,
        out_specs=[VMEM] * len(MADE),
        scratch_shapes=[pltpu.VMEM(turned_shape(MIDDLE_RING, ny, nz), F32)] * 2,
        compiler_params=pltpu.CompilerParams(vmem_limit_bytes=5 * 2**20),
        cost_estimate=pl.CostEstimate(flops=40 * nx * ny * nz, bytes_accessed=16 * nx * ny * nz, transcendentals=0),
        name="middle",
    )(*own)


def made_place(middles, ends, n, name, i, end, j):
    if 0 < j < n - 1:
        return middles[name], i, ROWS * j
    return ends[name], end, ROWS * {0: 0, n - 1: 1, n: 2}[j]


def inner_kernel(e, m, r, eh, mh, rh, *rest):
    nx, ny, nz = e.shape
    n = ny // ROWS
    own = {"e": (e, eh), "m": (m, mh), "r": (r, rh)}
    count = len(MADE)
    middles, rest = dict(zip(MADE, rest)), rest[count:]
    out_hbm, out, handed, rest = rest[0], rest[1], dict(zip(MADE, rest[2:])), rest[2 + count :]
    ends, rest = dict(zip(MADE, rest)), rest[count:]
    rings, (sem,) = dict(zip(TURNED1 + TURNED2, rest)), rest[4:]

    def place(name, i, j):
        if name in own:
            ref, strip = own[name]
            return (strip, number(i), 0) if j == n else (ref, number(i), ROWS * j)
        return made_place(middles, ends, n, name, number(i), i.slot, j)

    slab = Slab(place, lambda name, i: (rings[name], i.slot), ny, nz, row_mask())
    around = [0, 1, n - 2, n - 1, n]
    ahead, behind = RING // 2, 3

    def send_out(first, count):
        at = pl.ds(first, count)
        return pltpu.make_async_copy(out.at[at], out_hbm.at[at], sem)

    def second(i):
        return slab.second(i, out, number(i))

    def first(i):
        return [
            slab.first(i, [0, n - 1, n]),
            slab.load(i.load(ahead, nx - 2), around, TURNED1),
            slab.load(i - 1, range(n + 1), TURNED2),
        ]

    def hand(k, slot):
        for name in MADE:
            handed[name][k] = ends[name][slot]

    for k in range(ahead):
        run(slab.load(Plane(1 + k, k), around, TURNED1))
    for k in range(RING):
        i = Plane(1 + k, k)
        if i.number < 2 + behind:
            run(*first(i)[: 2 if k == 0 else 3])
        else:
            run(second(i - behind), *first(i))
    hand(0, 0)
    hand(1, 1)
    send_out(2, 2).start()

    @pl.loop(1, (nx - 2) // RING)
    def _(t):
        @pl.when(t > 1)
        def _():
            send_out(4 + RING * (t - 2), RING).start()

        for k in range(RING):
            i = Plane(1 + RING * t + k, k)
            run(second(i - behind), *first(i))

    hand(2, (nx - 4) % RING)
    hand(3, (nx - 3) % RING)
    for i in (nx - 4, nx - 3):
        run(second(Plane(i, i - 1)))
    send_out(2, unsent(nx) - 2).wait()


def unsent(nx):
    return max(4, nx - 4 - RING)


def inner(own, strips, middles):
    nx, ny, nz = own[0].shape
    args = (*own, *strips, *middles)
    return pl.pallas_call(
        inner_kernel,
        out_shape=[jax.ShapeDtypeStruct((nx, ny, nz), F32)] * 2
        + [jax.ShapeDtypeStruct((4, 3 * ROWS, nz), F32)] * len(MADE),
        in_specs=[VMEM] * len(args),
        out_specs=[HBM] + [VMEM] * (1 + len(MADE)),
        scratch_shapes=[pltpu.VMEM((RING, 3 * ROWS, nz), F32)] * len(MADE)
        + [pltpu.VMEM(turned_shape(RING, ny, nz), F32)] * 4
        + [pltpu.SemaphoreType.DMA],
        compiler_params=pltpu.CompilerParams(vmem_limit_bytes=7 * 2**20),
        cost_estimate=pl.CostEstimate(flops=40 * nx * ny * nz, bytes_accessed=16 * nx * ny * nz, transcendentals=0),
        name="inner",
    )(*args)


def outer_kernel(e, m, r, eh, mh, rh, got_out, got_back, corner_out, corner_back, second, *rest):
    nx, ny, nz = e.shape
    n = ny // ROWS
    count = len(MADE)
    middles, ends, rest = dict(zip(MADE, rest)), dict(zip(MADE, rest[count:])), rest[2 * count + 1 :]
    out_hbm, made, rest = rest[0], dict(zip(MADE, rest[1:])), rest[1 + count :]
    rings, (out, sems) = dict(zip(TURNED1 + TURNED2, rest)), rest[4:]
    own = {"e": e, "m": m, "r": r}
    strips = {"e": eh, "m": mh, "r": rh}
    got_at = {("e", -1): 0, ("m", -1): 1, ("m", -2): 2, ("r", -1): 3}
    corner_at = {"e": 0, "m": 1}
    mask = row_mask()
    late = pl.ds(unsent(nx), nx - 2 - unsent(nx))
    writes = [pltpu.make_async_copy(second.at[late], out_hbm.at[late], sems.at[4])]
    writes[0].start()
    sides = []
    for side, (got, corner) in enumerate(((got_out, corner_out), (got_back, corner_back))):
        low = sends_up(side == 1)
        there = jnp.where(low, has_prev("space"), has_next("space"))

        def at(q, low=low):
            return jnp.where(low, q, nx - 1 - q)

        def place(name, q, j, got=got, corner=corner, low=low, at=at, side=side):
            if name in own:
                if q >= 0:
                    return (strips[name], at(q), 0) if j == n else (own[name], at(q), ROWS * j)
                if j == n:
                    return corner, corner_at[name], 0
                return got, got_at[name, q], ROWS * j
            if q <= 0:
                return made[name], 2 * side + 1 + q, ROWS * j
            i = jnp.where(low, q, nx - 2 - q) if name == "cx" else at(q)
            end = jnp.where(low, q - 1, 3 - q if name == "cx" else 4 - q)
            return made_place(middles, ends, n, name, i, end, j)

        slab = Slab(place, lambda name, q, side=side: (rings[name], 2 * side + q % 2), ny, nz, mask)
        keep = jnp.broadcast_to(jnp.where(there, 1, 0), (ROWS, LANES)) == 1
        sides.append((slab, keep, at))

    def both(call):
        run(*(call(slab, keep) for slab, keep, _ in sides))

    both(lambda slab, _: slab.load(-1, range(n + 1), TURNED1))
    both(lambda slab, _: slab.load(0, range(n + 1), TURNED1))
    both(lambda slab, _: slab.load(1, range(n + 1), TURNED2))
    both(lambda slab, keep: slab.first(-1, range(n), keep=keep, e_before=False))
    both(lambda slab, _: slab.first(0, range(n + 1)))
    both(lambda slab, _: slab.load(0, range(n + 1), TURNED2))
    for q in (0, 1):
        for side, (slab, _, at) in enumerate(sides):
            run(slab.second(q, out, 2 * side + q))
            c = pltpu.make_async_copy(out.at[2 * side + q], out_hbm.at[at(q)], sems.at[2 * side + q])
            c.start()
            writes.append(c)
    for c in writes:
        c.wait()


def outer(own, strips, got, corners, second, middles, ends, out):
    nx, ny, nz = own[0].shape
    args = (*own, *strips, *got, *corners, second, *middles, *ends)
    return pl.pallas_call(
        outer_kernel,
        out_shape=jax.ShapeDtypeStruct((nx, ny, nz), F32),
        in_specs=[VMEM] * len(args) + [HBM],
        out_specs=HBM,
        input_output_aliases={len(args): 0},
        scratch_shapes=[pltpu.VMEM((4, ny + ROWS, nz), F32)] * len(MADE)
        + [pltpu.VMEM(turned_shape(4, ny, nz), F32)] * 4
        + [pltpu.VMEM((4, ny, nz), F32), pltpu.SemaphoreType.DMA((5,))],
        compiler_params=pltpu.CompilerParams(vmem_limit_bytes=8 * 2**20),
        name="outer",
    )(*args, out)


def shards(residual, mobility, initial_guess):
    own = (initial_guess, mobility, residual)
    *rows, plane_out, plane_back = send(*(pltpu.with_memory_space_constraint(v, pltpu.HBM) for v in own))
    got = [along_space(v, back) for v, back in ((plane_out, False), (plane_back, True))]
    rows = [along_member(v, back) for v, back in zip(rows, (False, True))]
    middles = middle(own)
    *strips, corner_out, corner_back = halo(*rows, residual.shape[0], middles[-1])
    corners = [along_space(v, back) for v, back in ((corner_out, False), (corner_back, True))]
    out, second, *ends = inner(own, strips, middles)
    return outer(own, strips, got, corners, second, middles, ends, out)


def solution(mesh):
    placed = P("space", "member", None)
    return jax.shard_map(shards, mesh=mesh, in_specs=(placed,) * 3, out_specs=placed, check_vma=False)
```
